32 devices in a mesh: dp: 8 (over y, x, core), owner: 4 (over z).
Axes of the slice: x: 2, y: 2, z: 4, core: 2. Of those that a mesh axis runs over, the one named last changes fastest.
Arguments:
- inputs: bfloat16 [32, 1024, 1536], P(('dp', 'owner')), may hold values from -6 to 6
- cotangent: bfloat16 [32, 1024, 1536], P(('dp', 'owner')), may hold values from -6 to 6
- lengths: int32 [32], replicated, may hold values from 1 to 1024, 16384 in all
- balance: int32 [32], replicated, may hold values from 0 to 31, each once
- owner_slot_tile: int32 [1920], replicated, may hold values from 0 to 1919, as said below
- master: float32 [1920, 128, 128], P(('dp', 'owner'))
- first_moment: float32 [1920, 128, 128], P(('dp', 'owner'))
- second_moment: float32 [1920, 128, 128], P(('dp', 'owner')), as said below
- left_basis: float32 [1920, 128, 128], P(('dp', 'owner')), as said below
- right_basis: float32 [1920, 128, 128], P(('dp', 'owner')), as said below
- left_stat: float32 [1920, 128, 128], P(('dp', 'owner')), as said below
- right_stat: float32 [1920, 128, 128], P(('dp', 'owner')), as said below
- small_master: float32 [19456], P(('dp', 'owner'))
- small_first: float32 [19456], P(('dp', 'owner'))
- small_second: float32 [19456], P(('dp', 'owner')), as said below
Outputs:
- activation: bfloat16 [32, 1024, 1536], P(('dp', 'owner'))
- input_grad: bfloat16 [32, 1024, 1536], P(('dp', 'owner'))
- new_master: float32 [1920, 128, 128], P(('dp', 'owner'))
- new_first: float32 [1920, 128, 128], P(('dp', 'owner'))
- new_second: float32 [1920, 128, 128], P(('dp', 'owner'))
- new_left: float32 [1920, 128, 128], P(('dp', 'owner'))
- new_right: float32 [1920, 128, 128], P(('dp', 'owner'))
- new_left_stat: float32 [1920, 128, 128], P(('dp', 'owner'))
- new_right_stat: float32 [1920, 128, 128], P(('dp', 'owner'))
- small_new: float32 [19456], P(('dp', 'owner'))
- small_first_new: float32 [19456], P(('dp', 'owner'))
- small_second_new: float32 [19456], P(('dp', 'owner'))
The draws below stay inside these ranges and needn't reach their ends.
Inputs may be any that keep to these rules, and one draw needn't show every extreme that they name: Each value once; slot s holds tile owner_slot_tile[s], values 1904 or more mark empty slots. `balance`: each sequence once. `lengths`: the longest sequence has exactly 1024 live positions. `left_basis`: each tile is orthogonal. `right_basis`: each tile is orthogonal. `left_stat`: each tile is symmetric with a positive, strictly dominant diagonal. `right_stat`: each tile is symmetric with a positive, strictly dominant diagonal. `second_moment`: positive. `small_second`: positive.
All inputs are finite; a program needn't handle non-finite values.
Results may differ from the reference program's by a relative error of at most 0.011.
The reference program's roundings to bfloat16 on the way count: a program that leaves them out, or rounds other values in their place, can miss the bound.
Values may be sent and summed in bfloat16 or wider, within the bound.
No kernel may reach another device: no remote copies, remote signals or barrier semaphores. Data moves between devices by JAX's collectives and lax.ppermute only.
A program may use at most 704 MiB of HBM per device.

```python
import math
import jax
import jax.numpy as jnp
import numpy as np
from jax import lax

D = 1536
R = 2048
F = 4608
KW = 4
TILE_EDGE_SIZE = 128
L = 1024
STEP = 5
NSEQ = 32
NT = 1904
SLOT_TOTAL = 1920
NSMALL = 19456


def slot_tiles(key):
    return jax.random.permutation(key, SLOT_TOTAL).astype(jnp.int32)


def grad_size():
    return math.sqrt(0.075 * NSEQ * L)


def small_size():
    return math.sqrt(0.5 * NSEQ * L)


def tile_spread(order):
    across = D // TILE_EDGE_SIZE * (R // TILE_EDGE_SIZE)
    wide_count = D // TILE_EDGE_SIZE * (F // TILE_EDGE_SIZE)
    head_count = R // TILE_EDGE_SIZE
    mark_two = 3 * across + 2 * head_count
    limits = [across, 2 * across, 3 * across, 3 * across + head_count, mark_two, mark_two + wide_count, mark_two + 2 * wide_count, mark_two + 3 * wide_count]
    scales = [D ** (-0.5), D ** (-0.5), 3.0 * R ** (-0.5), TILE_EDGE_SIZE ** (-0.5), TILE_EDGE_SIZE ** (-0.5), D ** (-0.5), D ** (-0.5), 2.0 * F ** (-0.5)]
    spread = jnp.full(order.shape, 0.03, jnp.float32)
    for bound_at, scale_at in zip(limits[::-1], scales[::-1]):
        spread = jnp.where(order < bound_at, scale_at, spread)
    return spread


def unit_rows(raw_vals):
    return raw_vals / jnp.sqrt(jnp.sum(raw_vals * raw_vals, axis=-1, keepdims=True))


def reflect_pair(first_moment_raw, second_moment_raw):
    first_unit = unit_rows(first_moment_raw)
    second_unit = unit_rows(second_moment_raw)
    inner = jnp.sum(first_unit * second_unit, axis=-1)[:, None, None]
    eye_tile = jnp.eye(TILE_EDGE_SIZE, dtype=jnp.float32)[None, :, :]
    first_outer = first_unit[:, :, None] * first_unit[:, None, :]
    second_outer = second_unit[:, :, None] * second_unit[:, None, :]
    cross_outer = first_unit[:, :, None] * second_unit[:, None, :]
    return eye_tile - 2.0 * first_outer - 2.0 * second_outer + 4.0 * inner * cross_outer


def stat_from(noise_values, diagonal_entries):
    eye_tile = jnp.eye(TILE_EDGE_SIZE, dtype=jnp.float32)
    symmetric = (noise_values + jnp.swapaxes(noise_values, 1, 2)) * (0.2 / TILE_EDGE_SIZE)
    body_vals = symmetric * (1.0 - eye_tile) + eye_tile * diagonal_entries[:, :, None]
    return body_vals * (TILE_EDGE_SIZE * grad_size() ** 2)


def draw_owner_slot_tile(key, part):
    return slot_tiles(key)


def draw_master(key, part):
    order = slot_tiles(key)
    key = jax.random.fold_in(key, 11)
    spread = tile_spread(order)[:, None, None]
    noise_values = jax.random.normal(key, (SLOT_TOTAL, TILE_EDGE_SIZE, TILE_EDGE_SIZE), jnp.float32)
    return noise_values * spread


def draw_first_moment(key, part):
    key = jax.random.fold_in(key, 12)
    noise_values = jax.random.normal(key, (SLOT_TOTAL, TILE_EDGE_SIZE, TILE_EDGE_SIZE), jnp.float32)
    return noise_values * grad_size()


def draw_second_moment(key, part):
    key = jax.random.fold_in(key, 13)
    cholesky_factor = jnp.exp(jax.random.uniform(key, (SLOT_TOTAL, TILE_EDGE_SIZE, TILE_EDGE_SIZE), jnp.float32, math.log(0.5), math.log(8.0)))
    return cholesky_factor * (grad_size() ** 2 * 0.4 / 0.6)


def draw_left_basis(key, part):
    key = jax.random.fold_in(key, 14)
    random_keys = jax.random.split(key, 2)
    first_moment_raw = jax.random.normal(random_keys[0], (SLOT_TOTAL, TILE_EDGE_SIZE), jnp.float32)
    second_moment_raw = jax.random.normal(random_keys[1], (SLOT_TOTAL, TILE_EDGE_SIZE), jnp.float32)
    return reflect_pair(first_moment_raw, second_moment_raw)


def draw_right_basis(key, part):
    key = jax.random.fold_in(key, 15)
    random_keys = jax.random.split(key, 2)
    first_moment_raw = jax.random.normal(random_keys[0], (SLOT_TOTAL, TILE_EDGE_SIZE), jnp.float32)
    second_moment_raw = jax.random.normal(random_keys[1], (SLOT_TOTAL, TILE_EDGE_SIZE), jnp.float32)
    return reflect_pair(first_moment_raw, second_moment_raw)


def draw_left_stat(key, part):
    key = jax.random.fold_in(key, 16)
    random_keys = jax.random.split(key, 2)
    noise_values = jax.random.uniform(random_keys[0], (SLOT_TOTAL, TILE_EDGE_SIZE, TILE_EDGE_SIZE), jnp.float32, -1.0, 1.0)
    diagonal_entries = jnp.exp(jax.random.uniform(random_keys[1], (SLOT_TOTAL, TILE_EDGE_SIZE), jnp.float32, 0.0, math.log(4.0)))
    return stat_from(noise_values, diagonal_entries)


def draw_right_stat(key, part):
    key = jax.random.fold_in(key, 17)
    random_keys = jax.random.split(key, 2)
    noise_values = jax.random.uniform(random_keys[0], (SLOT_TOTAL, TILE_EDGE_SIZE, TILE_EDGE_SIZE), jnp.float32, -1.0, 1.0)
    diagonal_entries = jnp.exp(jax.random.uniform(random_keys[1], (SLOT_TOTAL, TILE_EDGE_SIZE), jnp.float32, 0.0, math.log(4.0)))
    return stat_from(noise_values, diagonal_entries)


def draw_small_master(key, part):
    key = jax.random.fold_in(key, 31)
    random_keys = jax.random.split(key, 2)
    index = jnp.arange(NSMALL)
    flat_part = jax.random.uniform(random_keys[1], (NSMALL,), jnp.float32)
    normal_part = jax.random.normal(random_keys[0], (NSMALL,), jnp.float32)
    decays = 0.5 + 5.5 * flat_part
    gains = 0.6 + 0.8 * flat_part
    taps = 0.5 * normal_part
    return jnp.where(index < 2 * D, gains, jnp.where(index < 2 * D + (KW + 3) * R, taps, decays))


def draw_small_first(key, part):
    key = jax.random.fold_in(key, 32)
    noise_values = jax.random.normal(key, (NSMALL,), jnp.float32)
    return noise_values * small_size()


def draw_small_second(key, part):
    key = jax.random.fold_in(key, 33)
    cholesky_factor = jnp.exp(jax.random.uniform(key, (NSMALL,), jnp.float32, math.log(0.5), math.log(8.0)))
    return cholesky_factor * (small_size() ** 2 * 0.4 / 0.6)


def block_scale(stream_key, shape, shards, smallest, top_value):
    def one(axis_at, shards_of):
        draws = jax.random.uniform(jax.random.fold_in(jax.random.fold_in(stream_key, 6), axis_at), (shards_of,), jnp.float32, smallest / len(shards), top_value / len(shards))
        return jnp.repeat(jnp.exp(draws), shape[axis_at] // shards_of).reshape((-1,) + (1,) * (len(shape) - axis_at - 1))

    loudness = one(*shards[0])
    for cut in shards[1:]:
        loudness = loudness * one(*cut)
    return loudness


def length_profile(count, total, reach, skew):
    loads = [(1 << 20) // math.isqrt(rank ** skew) + 1 for rank in range(2, count + 1)]
    spare, given = total - reach - (count - 1), [1] * (count - 1)
    while spare > 0:
        free = [i for i in range(count - 1) if given[i] < reach]
        mass, budget = sum([loads[i] for i in free]), spare
        for i in free:
            addition = min(reach - given[i], max(1, budget * loads[i] // mass), spare)
            given[i] = given[i] + addition
            spare = spare - addition
    return np.array([reach] + given)


def ragged_sizes(own_key, number_of, total, most, skew):
    if number_of == 2:
        one = jax.random.randint(own_key, (), max(1, total - most), min(most, total - 1) + 1)
        return jnp.stack([one, total - one])
    sizes = jnp.asarray(length_profile(number_of, total, most, skew), jnp.int32)
    twos = (number_of - 1) // 2
    donor, receiver = sizes[1:1 + 2 * twos:2], sizes[2:2 + 2 * twos:2]
    room = jnp.minimum(donor - 1, most - receiver)
    moved = jax.random.randint(jax.random.fold_in(own_key, 1), (twos,), 0, 1 << 20) % (room + 1)
    sizes = sizes.at[1:1 + 2 * twos:2].set(donor - moved).at[2:2 + 2 * twos:2].set(receiver + moved)
    return sizes[jax.random.permutation(jax.random.fold_in(own_key, 2), number_of)]


def bell_draw(own_key, shape, scale, bound, pieces=(), kind=jnp.bfloat16):
    values = scale * jax.random.normal(own_key, shape, jnp.float32)
    if pieces:
        values = values * block_scale(own_key, shape, pieces, -0.22, 0.18)
    return jnp.clip(values, -bound, bound).astype(kind)


def setup_inputs(seed: int = 0) -> dict:
    splits = jax.random.split(jax.random.key(seed), 16)
    inputs = bell_draw(splits[0], (NSEQ, L, D), 1.0, 6.0, ((0, 32),))
    cotangent = bell_draw(splits[1], (NSEQ, L, D), 1.0, 6.0, ((0, 32),))
    lengths = ragged_sizes(splits[2], NSEQ, NSEQ * L // 2, L, 2).astype(jnp.int32)
    balance = jax.random.permutation(splits[3], NSEQ).astype(jnp.int32)
    owner_slot_tile = draw_owner_slot_tile(jax.random.fold_in(splits[15], 71), 0)
    master = draw_master(jax.random.fold_in(splits[15], 71), 0)
    first_moment = draw_first_moment(jax.random.fold_in(splits[15], 71), 0)
    second_moment = draw_second_moment(jax.random.fold_in(splits[15], 71), 0)
    left_basis = draw_left_basis(jax.random.fold_in(splits[15], 71), 0)
    right_basis = draw_right_basis(jax.random.fold_in(splits[15], 71), 0)
    left_stat = draw_left_stat(jax.random.fold_in(splits[15], 71), 0)
    right_stat = draw_right_stat(jax.random.fold_in(splits[15], 71), 0)
    small_master = draw_small_master(jax.random.fold_in(splits[15], 71), 0)
    small_first = draw_small_first(jax.random.fold_in(splits[15], 71), 0)
    small_second = draw_small_second(jax.random.fold_in(splits[15], 71), 0)
    return dict(inputs=inputs, cotangent=cotangent, lengths=lengths, balance=balance, owner_slot_tile=owner_slot_tile, master=master, first_moment=first_moment, second_moment=second_moment, left_basis=left_basis, right_basis=right_basis, left_stat=left_stat, right_stat=right_stat, small_master=small_master, small_first=small_first, small_second=small_second)


EPS = 1e-06
BETA_ONE = 0.5
BETA_TWO = 0.6
BETA_STAT = 0.5
RATE = 0.02
SMALL_RATE = 0.6
DECAY = 0.01
ADAM_EPS = 1e-08
HIGH = lax.Precision.HIGHEST

@jax.custom_vjp
def low(v):
    return lax.optimization_barrier(v.astype(jnp.bfloat16)).astype(jnp.float32)

@jax.custom_vjp
def low_back(v):
    return v

def low_keep(v):
    return (low(v), None)

def low_pass(kept, grad):
    return (grad,)

def back_keep(v):
    return (v, None)

def back_low(kept, grad):
    return (low(grad),)
low.defvjp(low_keep, low_pass)
low_back.defvjp(back_keep, back_low)

def rms_norm(values, scales):
    return values * lax.rsqrt(lax.optimization_barrier(jnp.mean(values * values, axis=-1, keepdims=True)) + EPS) * scales

def causal_conv(values, kernel, shift_bias):
    length_now = values.shape[-2]
    total = shift_bias + kernel[0] * values
    for offset in range(1, kernel.shape[0]):
        padding = [(0, 0)] * (values.ndim - 2) + [(offset, 0), (0, 0)]
        total = total + kernel[offset] * jnp.pad(values, padding)[..., :length_now, :]
    return total

def lru_gates(rec_pre, inp_pre, conv_vals, rec_bias, inp_bias, decay_log):
    recall = jax.nn.sigmoid(rec_pre + rec_bias)
    admitted = jax.nn.sigmoid(inp_pre + inp_bias)
    log_keep = -8.0 * recall * jax.nn.softplus(-decay_log)
    return (jnp.exp(log_keep), jnp.sqrt(-jnp.expm1(2.0 * log_keep)) * admitted * conv_vals)

def combine(earlier, later):
    return (earlier[0] * later[0], later[0] * earlier[1] + later[1])

def mixgate(states, pre_vals):
    return states * jax.nn.gelu(pre_vals)

def gelu_gate(gate_vals, up_vals):
    return jax.nn.gelu(gate_vals) * up_vals

def untile(blocks, row_count, col_count):
    tile_edge = blocks.shape[-1]
    shaped = blocks.reshape(row_count // tile_edge, col_count // tile_edge, tile_edge, tile_edge)
    return shaped.transpose(0, 2, 1, 3).reshape(row_count, col_count)

def tiles_of(matrix, tile_edge):
    row_count, col_count = matrix.shape
    shaped = matrix.reshape(row_count // tile_edge, tile_edge, col_count // tile_edge, tile_edge)
    return shaped.transpose(0, 2, 1, 3).reshape(-1, tile_edge, tile_edge)

def split_tiles(tiles):
    tile_edge = tiles.shape[-1]
    across = D // tile_edge * (R // tile_edge)
    wide_count = D // tile_edge * (F // tile_edge)
    head_count = R // tile_edge
    mark_one = 3 * across
    mark_two = mark_one + 2 * head_count
    w_x = untile(tiles[0:across], D, R)
    w_y = untile(tiles[across:2 * across], D, R)
    w_out = untile(tiles[2 * across:mark_one], R, D)
    w_rec = tiles[mark_one:mark_one + head_count]
    w_inp = tiles[mark_one + head_count:mark_two]
    w_gate = untile(tiles[mark_two:mark_two + wide_count], D, F)
    w_up = untile(tiles[mark_two + wide_count:mark_two + 2 * wide_count], D, F)
    w_down = untile(tiles[mark_two + 2 * wide_count:mark_two + 3 * wide_count], F, D)
    return (w_x, w_y, w_out, w_rec, w_inp, w_gate, w_up, w_down)

def split_small(vector):
    offset_base = 2 * D + KW * R
    gain_one = vector[0:D]
    gain_two = vector[D:2 * D]
    conv_kernel = vector[2 * D:offset_base].reshape(KW, R)
    conv_bias = vector[offset_base:offset_base + R]
    rec_bias = vector[offset_base + R:offset_base + 2 * R]
    inp_bias = vector[offset_base + 2 * R:offset_base + 3 * R]
    decay_log = vector[offset_base + 3 * R:offset_base + 4 * R]
    return (gain_one, gain_two, conv_kernel, conv_bias, rec_bias, inp_bias, decay_log)

def orthonormal(matrix):
    gram_matrix = jnp.einsum('nki,nkj->nij', matrix, matrix, precision=HIGH)
    lower_factor = lax.linalg.cholesky(gram_matrix)
    return lax.linalg.triangular_solve(lower_factor, matrix, left_side=False, lower=True, transpose_a=True)

def rotate_step(grads, weights, first_vals, second_vals, left_vals, right_vals, left_stats, right_stats):
    half_turn = jnp.einsum('nki,nkl->nil', left_vals, grads, precision=HIGH)
    turned = jnp.einsum('nil,nlj->nij', half_turn, right_vals, precision=HIGH)
    first_new = BETA_ONE * first_vals + (1.0 - BETA_ONE) * turned
    second_new = BETA_TWO * second_vals + (1.0 - BETA_TWO) * turned * turned
    scaled = first_new / (1.0 - BETA_ONE ** STEP) / (jnp.sqrt(second_new / (1.0 - BETA_TWO ** STEP)) + ADAM_EPS)
    back_half = jnp.einsum('nik,nkl->nil', left_vals, scaled, precision=HIGH)
    update = jnp.einsum('nil,njl->nij', back_half, right_vals, precision=HIGH)
    weight_new = weights - RATE * (update + DECAY * weights)
    left_stat_new = BETA_STAT * left_stats + (1.0 - BETA_STAT) * jnp.einsum('nik,njk->nij', grads, grads, precision=HIGH)
    right_stat_new = BETA_STAT * right_stats + (1.0 - BETA_STAT) * jnp.einsum('nki,nkj->nij', grads, grads, precision=HIGH)
    left_new = orthonormal(jnp.einsum('nik,nkj->nij', left_stat_new, left_vals, precision=HIGH))
    right_new = orthonormal(jnp.einsum('nik,nkj->nij', right_stat_new, right_vals, precision=HIGH))
    return (weight_new, first_new, second_new, left_new, right_new, left_stat_new, right_stat_new)

def small_step(grads, weights, first_vals, second_vals):
    first_new = BETA_ONE * first_vals + (1.0 - BETA_ONE) * grads
    second_new = BETA_TWO * second_vals + (1.0 - BETA_TWO) * grads * grads
    scaled = first_new / (1.0 - BETA_ONE ** STEP) / (jnp.sqrt(second_new / (1.0 - BETA_TWO ** STEP)) + ADAM_EPS)
    return (weights - SMALL_RATE * scaled, first_new, second_new)

def block_mul(values, blocks):
    head_count, tile_edge = (blocks.shape[0], blocks.shape[1])
    shaped = values.reshape(values.shape[:-1] + (head_count, tile_edge))
    product = jnp.einsum('...hi,hij->...hj', shaped, blocks, precision=HIGH)
    return product.reshape(values.shape)

def layer(weights, small_vals, tokens):
    w_x, w_y, w_out, w_rec, w_inp, w_gate, w_up, w_down = weights
    gain_one, gain_two, conv_kernel, conv_bias, rec_bias, inp_bias, decay_log = split_small(small_vals)
    normed_one = low(rms_norm(tokens, gain_one))
    branch = low_back(jnp.dot(normed_one, w_x, precision=HIGH))
    gate_pre = low_back(jnp.dot(normed_one, w_y, precision=HIGH))
    conv_out = low(causal_conv(branch, conv_kernel, conv_bias))
    rec_pre = low_back(block_mul(conv_out, w_rec))
    inp_pre = low_back(block_mul(conv_out, w_inp))
    decays, driven = lru_gates(rec_pre, inp_pre, conv_out, rec_bias, inp_bias, decay_log)
    states = lax.associative_scan(combine, (decays, driven), axis=decays.ndim - 2)[1]
    mixed = low(mixgate(states, gate_pre))
    resid = tokens + low_back(jnp.dot(mixed, w_out, precision=HIGH))
    normed_two = low(rms_norm(resid, gain_two))
    gate_act = low_back(jnp.dot(normed_two, w_gate, precision=HIGH))
    up_act = low_back(jnp.dot(normed_two, w_up, precision=HIGH))
    glu_out = low(gelu_gate(gate_act, up_act))
    return resid + low_back(jnp.dot(glu_out, w_down, precision=HIGH))

def reference(inputs, cotangent, lengths, balance, owner_slot_tile, master, first_moment, second_moment, left_basis, right_basis, left_stat, right_stat, small_master, small_first, small_second):
    slot_indices = jnp.arange(SLOT_TOTAL, dtype=jnp.int32)
    slot_lookup = jnp.zeros((SLOT_TOTAL,), jnp.int32).at[owner_slot_tile].set(slot_indices)
    held = lax.optimization_barrier(master.astype(jnp.bfloat16)).astype(jnp.float32)
    small_held = lax.optimization_barrier(small_master.astype(jnp.bfloat16)).astype(jnp.float32)
    weights = split_tiles(held[slot_lookup[:NT]])
    place = jnp.zeros((NSEQ,), jnp.int32).at[balance].set(jnp.arange(NSEQ, dtype=jnp.int32))
    given_back = cotangent[place].astype(jnp.float32)
    positions = jnp.arange(L, dtype=jnp.int32)

    def one_sequence(running, sequence_item):
        tokens, back_vals, length_one = sequence_item
        live_mask = (positions < length_one).astype(jnp.float32)[:, None]
        result, pull_back = jax.vjp(layer, weights, small_held, tokens.astype(jnp.float32))
        grad_weights, grad_small, grad_tokens = pull_back(back_vals * live_mask)
        total_weights = tuple((earlier_sum + new_part for earlier_sum, new_part in zip(running[0], grad_weights)))
        return ((total_weights, running[1] + grad_small), (result.astype(jnp.bfloat16), grad_tokens.astype(jnp.bfloat16)))
    initial = (tuple((jnp.zeros_like(weight_one) for weight_one in weights)), jnp.zeros_like(small_held))
    (totals, small_total), (activation, input_grad) = lax.scan(one_sequence, initial, (inputs, given_back, lengths))
    grad_x, grad_y, grad_out, grad_rec, grad_inp, grad_gate, grad_up, grad_down = totals
    grad_tiles = jnp.concatenate([tiles_of(grad_x, TILE_EDGE_SIZE), tiles_of(grad_y, TILE_EDGE_SIZE), tiles_of(grad_out, TILE_EDGE_SIZE), grad_rec, grad_inp, tiles_of(grad_gate, TILE_EDGE_SIZE), tiles_of(grad_up, TILE_EDGE_SIZE), tiles_of(grad_down, TILE_EDGE_SIZE)], axis=0)
    filled = (owner_slot_tile < NT)[:, None, None]
    slot_grads = jnp.where(filled, grad_tiles[jnp.minimum(owner_slot_tile, NT - 1)], 0.0)
    new_master, new_first, new_second, new_left, new_right, new_left_stat, new_right_stat = rotate_step(slot_grads, master, first_moment, second_moment, left_basis, right_basis, left_stat, right_stat)
    small_new, small_first_new, small_second_new = small_step(small_total, small_master, small_first, small_second)
    return (activation, input_grad, new_master, new_first, new_second, new_left, new_right, new_left_stat, new_right_stat, small_new, small_first_new, small_second_new)
```

```python
import functools
import math

import jax
import jax.numpy as jnp
from jax import lax
from jax.experimental import pallas as pl
from jax.experimental.pallas import tpu as pltpu
from jax.sharding import Mesh
from jax.sharding import PartitionSpec as P

D = 1536
R = 2048
F = 4608
KW = 4
STEP = 5
NT = 1904
E = 128

EPS = 1e-06
BETA_ONE = 0.5
BETA_TWO = 0.6
BETA_STAT = 0.5
RATE = 0.02
SMALL_RATE = 0.6
DECAY = 0.01
ADAM_EPS = 1e-08
HIGH = lax.Precision.HIGHEST

DT, RT, FT = D // E, R // E, F // E
AT_X = 0
AT_Y = DT * RT
AT_OUT = 2 * DT * RT
AT_REC = 3 * DT * RT
AT_INP = AT_REC + RT
AT_GATE = AT_INP + RT
AT_UP = AT_GATE + DT * FT
AT_DOWN = AT_UP + DT * FT

AXES = ("yx", "core", "owner")
BLOCK = 256
WIDE = BLOCK // E
FFN_BLOCK = 256
FFN_WIDE = FFN_BLOCK // E
CHUNK = 32
ROWS = 256
HIGH_ROWS = 512

BF = jnp.bfloat16
F32 = jnp.float32

NN = (((1,), (0,)), ((), ()))
NT_DIMS = (((1,), (1,)), ((), ()))
TN_DIMS = (((0,), (0,)), ((), ()))


def mm(left, right, dims=NN):
    return lax.dot_general(left, right, dims, preferred_element_type=F32)


def gelu_pair(x):
    c = math.sqrt(2.0 / math.pi)
    sq = x * x
    t = jnp.tanh(x * (c + (c * 0.044715) * sq))
    half = 0.5 + 0.5 * t
    slope = half + (0.5 * x) * (1.0 - t * t) * (c + (3.0 * c * 0.044715) * sq)
    return x * half, slope


def gelu_only(x):
    c = math.sqrt(2.0 / math.pi)
    return x * (0.5 + 0.5 * jnp.tanh(x * (c + (c * 0.044715) * (x * x))))


def minus_expm1(y, exp_y):
    poly = 1.0 + y * (1.0 / 7.0)
    for n in (6.0, 5.0, 4.0, 3.0, 2.0):
        poly = 1.0 + (y * (1.0 / n)) * poly
    return jnp.where(y > -0.35, -y * poly, 1.0 - exp_y)


def whole(shape):
    return pl.BlockSpec(shape, lambda *_: (0,) * len(shape), pipeline_mode=pl.Buffered(1))


ANY = pl.BlockSpec(memory_space=pl.ANY)


def wait_bytes(ref, sem):
    pltpu.make_async_copy(ref, ref, sem).wait()


def load_tile(pos, packed, tile, dst, row, col, sem):
    pltpu.make_async_copy(
        packed.at[pos[tile]], dst.at[pl.ds(row * E, E), pl.ds(col * E, E)], sem
    ).start()


def store_tile(pos, packed, tile, src, row, col, sem):
    pltpu.make_async_copy(
        src.at[pl.ds(row * E, E), pl.ds(col * E, E)], packed.at[pos[tile]], sem
    ).start()


def move_pair(move, pos, packed, ref, sem, firsts, across, row, wide=WIDE):
    for m, first in enumerate(firsts):
        for c in range(wide):
            move(pos, packed, first + row * across + c, ref, row, m * wide + c, sem)


def move_down(move, pos, packed, ref, sem, first, col, wide=WIDE):
    for r in range(wide):
        move(pos, packed, first + r * DT + col, ref, r, col, sem)


def move_heads(move, pos, packed, ref, sem, step):
    for h in range(WIDE):
        for base, col in ((AT_REC, 0), (AT_INP, 1)):
            move(pos, packed, base + step * WIDE + h, ref.at[h], 0, col, sem)


def load_xy(pos, packed, wxy, wo, sem, step, begin, count):
    at = step * WIDE
    for i in range(count):
        move_pair(load_tile, pos, packed, wxy, sem, (AT_X + at, AT_Y + at), RT, begin + i)
        move_down(load_tile, pos, packed, wo, sem, AT_OUT + at * DT, begin + i)


def wait_xy(wxy, wo, wri, sem):
    wait_bytes(wxy, sem)
    wait_bytes(wo, sem)
    wait_bytes(wri, sem)


def conv_chunk(ref, r, taps, bias):
    now = ref[pl.ds(r, CHUNK), :]
    before = ref[pl.ds(pl.multiple_of(jnp.maximum(r - 8, 0), 8), 8), :]
    ext = jnp.concatenate([jnp.where(r == 0, 0.0, before), now], axis=0)
    total = bias + taps[0:1] * now
    for k in range(1, KW):
        total = total + taps[k : k + 1] * ext[8 - k : 8 - k + CHUNK]
    return total


def heads_of(pre, part):
    return jnp.concatenate(
        [pre[:, h * 2 * E + part * E : h * 2 * E + (part + 1) * E] for h in range(WIDE)], axis=1
    )


def scan_chunk(a, b, carry, reverse):
    groups = CHUNK // 8
    shape = (groups, 8, a.shape[-1])
    a, b = a.reshape(shape), b.reshape(shape)
    row = lax.broadcasted_iota(jnp.int32, shape, 1)
    for d in (1, 2, 4):
        turn = 8 - d if reverse else d
        ok = row < 8 - d if reverse else row >= d
        a_far = pltpu.roll(a, turn, 1)
        b_far = pltpu.roll(b, turn, 1)
        b = b + a * jnp.where(ok, b_far, 0.0)
        a = a * jnp.where(ok, a_far, 1.0)
    out = [None] * groups
    for g in range(groups)[:: -1 if reverse else 1]:
        out[g] = b[g] + a[g] * carry
        carry = out[g][0:1] if reverse else out[g][7:8]
    return jnp.concatenate(out, axis=0), carry


def norm_rows(x):
    return lax.rsqrt(jnp.mean(x * x, axis=-1, keepdims=True) + EPS)


def temporal_forward_kernel(
    pos, packed, tokens, gain, params,
    branch, keep_out, u_out, p_out, q_out, ga_out, g_out, sg_out, conv_low, mixed, resid,
    normed, wxy, wo, wri, gate_pre, pre, sems,
):
    step = pl.program_id(0)
    last = pl.num_programs(0) - 1
    slot = lax.rem(step, 2)
    other = 1 - slot
    after = jnp.minimum(step + 1, last)
    length = tokens.shape[0]

    @pl.when(step == 0)
    def _():
        move_heads(load_tile, pos, packed, wri.at[0], sems.at[0], 0)
        load_xy(pos, packed, wxy.at[0], wo.at[0], sems.at[0], 0, 0, DT)

        def one(i, _):
            rows = pl.ds(pl.multiple_of(i * E, E), E)
            x = tokens[rows, :].astype(F32)
            normed[rows, :] = (x * norm_rows(x) * gain[...]).astype(BF)
            resid[rows, :] = x
            return 0

        lax.fori_loop(0, length // E, one, 0)

    wait_xy(wxy.at[slot], wo.at[slot], wri.at[slot], sems.at[slot])
    move_heads(load_tile, pos, packed, wri.at[other], sems.at[other], after)

    for c in range(length // HIGH_ROWS):
        rows = slice(c * HIGH_ROWS, (c + 1) * HIGH_ROWS)
        both = mm(normed[rows, :], wxy[slot])
        branch[rows, :] = both[:, :BLOCK]
        gate_pre[rows, :] = both[:, BLOCK:]
        half = DT // 2
        load_xy(pos, packed, wxy.at[other], wo.at[other], sems.at[other], after, c * half, half)
    values = params[...]

    def convolve(i, _):
        r = pl.multiple_of(i * CHUNK, CHUNK)
        conv_low[pl.ds(r, CHUNK), :] = conv_chunk(branch, r, values[0:4], values[4:5]).astype(BF)
        return 0

    lax.fori_loop(0, length // CHUNK, convolve, 0, unroll=2)
    for h in range(WIDE):
        pre[:, h * 2 * E : (h + 1) * 2 * E] = mm(conv_low[:, h * E : (h + 1) * E], wri[slot, h])

    row_in = lax.broadcasted_iota(jnp.int32, (CHUNK, BLOCK), 0)

    def recur(i, carry):
        rows = pl.ds(pl.multiple_of(i * CHUNK, CHUNK), CHUNK)
        recall = jax.nn.sigmoid(heads_of(pre[rows, :], 0) + values[5:6])
        admit = jax.nn.sigmoid(heads_of(pre[rows, :], 1) + values[6:7])
        log_keep = recall * values[7:8]
        keep = jnp.exp(log_keep)
        keep_sq = keep * keep
        gap = jnp.sqrt(minus_expm1(2.0 * log_keep, keep_sq))
        conv = conv_low[rows, :].astype(F32)
        ga = gap * admit
        driven = ga * conv
        state, carry_out = scan_chunk(keep, driven, carry, False)
        prior = jnp.where(row_in == 0, carry, pltpu.roll(state, 1, 0))
        g, slope = gelu_pair(gate_pre[rows, :])
        mixed[rows, :] = (state * g).astype(BF)
        g_out[rows, :] = g
        sg_out[rows, :] = state * slope
        keep_out[rows, :] = keep
        ga_out[rows, :] = ga
        q_out[rows, :] = driven * (1.0 - admit)
        u = (prior * keep - (admit * conv) * (keep_sq / gap)) * recall
        u_out[rows, :] = u
        p_out[rows, :] = u * ((1.0 - recall) * values[7:8])
        return carry_out

    lax.fori_loop(0, length // CHUNK, recur, jnp.zeros((1, BLOCK), F32), unroll=2)

    for c in range(D // ROWS):
        cols = slice(c * ROWS, (c + 1) * ROWS)
        resid[:, cols] += mm(mixed[...], wo[slot, :, cols])

    @pl.when(step == last)
    def _():
        wait_xy(wxy.at[other], wo.at[other], wri.at[other], sems.at[other])


def temporal_forward(pos, packed, tokens, gain, params):
    length = tokens.shape[0]
    column = pl.BlockSpec((length, BLOCK), lambda i, *_: (0, i))
    wide = jax.ShapeDtypeStruct((length, R), F32)
    low = jax.ShapeDtypeStruct((length, R), BF)
    *saved, resid = pl.pallas_call(
        temporal_forward_kernel,
        grid_spec=pltpu.PrefetchScalarGridSpec(
            num_scalar_prefetch=1,
            grid=(R // BLOCK,),
            in_specs=[
                ANY,
                whole((length, D)),
                whole((1, D)),
                pl.BlockSpec((16, BLOCK), lambda i, *_: (0, i)),
            ],
            out_specs=[column] * 10 + [whole((length, D))],
            scratch_shapes=[
                pltpu.VMEM((length, D), BF),
                pltpu.VMEM((2, D, 2 * BLOCK), BF),
                pltpu.VMEM((2, BLOCK, D), BF),
                pltpu.VMEM((2, WIDE, E, 2 * E), BF),
                pltpu.VMEM((length, BLOCK), F32),
                pltpu.VMEM((length, 2 * BLOCK), F32),
                pltpu.SemaphoreType.DMA((2,)),
            ],
        ),
        out_shape=[wide] * 8 + [low] * 2 + [jax.ShapeDtypeStruct((length, D), F32)],
        compiler_params=pltpu.CompilerParams(vmem_limit_bytes=56 << 20),
        cost_estimate=pl.CostEstimate(
            flops=2 * length * D * R * 3, bytes_accessed=110 << 20, transcendentals=6 * length * R
        ),
        name="temporal_forward",
    )(pos, packed, tokens, gain, params)
    return saved, resid


def load_ffn(pos, packed, wgu, wd, sem, step, begin, count):
    at = step * FFN_WIDE
    for i in range(count):
        move_pair(load_tile, pos, packed, wgu, sem, (AT_GATE + at, AT_UP + at), FT, begin + i, FFN_WIDE)
        move_down(load_tile, pos, packed, wd, sem, AT_DOWN + at * DT, begin + i, FFN_WIDE)


def ffn_kernel(
    pos, packed, resid, back, gain, grads, activation, resid_back, out_back, gain_grad,
    normed, normed_t, total, normed_back, wgu, wd, glu, gub, sgu, sd, low, load_sems, store_sems, sem,
):
    step = pl.program_id(0)
    last = pl.num_programs(0) - 1
    slot = lax.rem(step, 2)
    other = 1 - slot
    after = jnp.minimum(step + 1, last)
    length = resid.shape[0]

    @pl.when(step == 0)
    def _():
        load_ffn(pos, packed, wgu.at[0], wd.at[0], load_sems.at[0], 0, 0, DT)

        def one(i, _):
            rows = pl.ds(pl.multiple_of(i * E, E), E)
            x = resid[rows, :]
            n = x * norm_rows(x) * gain[...]
            normed[rows, :] = n.astype(BF)
            normed_t[:, rows] = n.T.astype(BF)
            total[rows, :] = x
            normed_back[rows, :] = jnp.zeros_like(x)
            return 0

        lax.fori_loop(0, length // E, one, 0)

    wait_bytes(wgu.at[slot], load_sems.at[slot])
    wait_bytes(wd.at[slot], load_sems.at[slot])

    for c in range(length // HIGH_ROWS):
        rows = slice(c * HIGH_ROWS, (c + 1) * HIGH_ROWS)
        acts = mm(normed[rows, :], wgu[slot])
        glu_back = mm(back[rows, :], wd[slot], NT_DIMS)
        up = acts[:, FFN_BLOCK:]
        g, slope = gelu_pair(acts[:, :FFN_BLOCK])
        glu[rows, :] = (g * up).astype(BF)
        gub[rows, :FFN_BLOCK] = (glu_back * up * slope).astype(BF)
        gub[rows, FFN_BLOCK:] = (glu_back * g).astype(BF)

    for c in range(D // ROWS):
        cols = slice(c * ROWS, (c + 1) * ROWS)
        total[:, cols] += mm(glu[...], wd[slot, :, cols])
        normed_back[:, cols] += mm(gub[...], wgu[slot, cols, :], NT_DIMS)
        load_ffn(pos, packed, wgu.at[other], wd.at[other], load_sems.at[other], after, c * 2, 2)

    @pl.when(step >= 2)
    def _():
        wait_bytes(sgu.at[slot], store_sems.at[slot])
        wait_bytes(sd.at[slot], store_sems.at[slot])

    at = step * FFN_WIDE
    out_sem = store_sems.at[slot]
    sd[slot] = mm(glu[...], back[...], TN_DIMS).astype(BF)
    for c in range(DT):
        move_down(store_tile, pos, grads, sd.at[slot], out_sem, AT_DOWN + at * DT, c, FFN_WIDE)
    half = D // 2
    for c in range(2):
        rows = slice(c * half, (c + 1) * half)
        sgu[slot, rows, :] = mm(normed_t[rows, :], gub[...]).astype(BF)
        for j in range(DT // 2):
            firsts = (AT_GATE + at, AT_UP + at)
            move_pair(store_tile, pos, grads, sgu.at[slot], out_sem, firsts, FT, c * (DT // 2) + j, FFN_WIDE)

    @pl.when(step == last)
    def _():
        def one(i, gain_sum):
            rows = pl.ds(pl.multiple_of(i * E, E), E)
            x = resid[rows, :]
            n_back = normed_back[rows, :]
            inv = norm_rows(x)
            scaled = n_back * gain[...]
            mean = jnp.mean(scaled * x, axis=-1, keepdims=True)
            x_back = back[rows, :].astype(F32) + (inv * scaled - x * (inv * inv * inv * mean))
            normed_back[rows, :] = x_back
            normed[rows, :] = x_back.astype(BF)
            low[rows, :] = total[rows, :].astype(BF)
            return gain_sum + jnp.sum((n_back * x * inv).reshape(E // 8, 8, D), axis=0)

        gain_sum = lax.fori_loop(0, length // E, one, jnp.zeros((8, D), F32))
        gain_grad[...] = jnp.sum(gain_sum, axis=0, keepdims=True)
        outs = [
            pltpu.make_async_copy(normed_back, resid_back, sem.at[0]),
            pltpu.make_async_copy(normed, out_back, sem.at[1]),
            pltpu.make_async_copy(low, activation, sem.at[2]),
        ]
        for copy in outs:
            copy.start()
        for copy in outs:
            copy.wait()
        wait_bytes(wgu.at[other], load_sems.at[other])
        wait_bytes(wd.at[other], load_sems.at[other])
        for s in range(2):
            wait_bytes(sgu.at[s], store_sems.at[s])
            wait_bytes(sd.at[s], store_sems.at[s])


def ffn(pos, packed, resid, back, gain):
    length = resid.shape[0]
    return pl.pallas_call(
        ffn_kernel,
        grid_spec=pltpu.PrefetchScalarGridSpec(
            num_scalar_prefetch=1,
            grid=(F // FFN_BLOCK,),
            in_specs=[ANY, whole((length, D)), whole((length, D)), whole((1, D))],
            out_specs=[ANY, ANY, ANY, ANY, whole((1, D))],
            scratch_shapes=[
                pltpu.VMEM((length, D), BF),
                pltpu.VMEM((D, length), BF),
                pltpu.VMEM((length, D), F32),
                pltpu.VMEM((length, D), F32),
                pltpu.VMEM((2, D, 2 * FFN_BLOCK), BF),
                pltpu.VMEM((2, FFN_BLOCK, D), BF),
                pltpu.VMEM((length, FFN_BLOCK), BF),
                pltpu.VMEM((length, 2 * FFN_BLOCK), BF),
                pltpu.VMEM((2, D, 2 * FFN_BLOCK), BF),
                pltpu.VMEM((2, FFN_BLOCK, D), BF),
                pltpu.VMEM((length, D), BF),
                pltpu.SemaphoreType.DMA((2,)),
                pltpu.SemaphoreType.DMA((2,)),
                pltpu.SemaphoreType.DMA((3,)),
            ],
        ),
        out_shape=[
            jax.ShapeDtypeStruct(packed.shape, BF),
            jax.ShapeDtypeStruct((length, D), BF),
            jax.ShapeDtypeStruct((length, D), F32),
            jax.ShapeDtypeStruct((length, D), BF),
            jax.ShapeDtypeStruct((1, D), F32),
        ],
        compiler_params=pltpu.CompilerParams(vmem_limit_bytes=60 << 20),
        cost_estimate=pl.CostEstimate(
            flops=18 * length * D * F, bytes_accessed=110 << 20, transcendentals=length * F
        ),
        name="ffn_both_ways",
    )(pos, packed, resid, back, gain)


def temporal_backward_kernel(
    pos, packed, grads_in, resid_back, tokens, out_back, gain, params,
    branch, keep_in, u_in, p_in, q_in, ga_in, g_in, sg_in, conv_low, mixed,
    grads, input_grad, gain_grad, small_grad,
    normed_t, normed_back, wxy, wo, wri, bp, ri, mixed_back, conv_back, resid_rows,
    sxy, so, sri, zeros, load_sems, store_sems, zero_sem, resid_sems,
):
    step = pl.program_id(0)
    last = pl.num_programs(0) - 1
    slot = lax.rem(step, 2)
    other = 1 - slot
    after = jnp.minimum(step + 1, last)
    length = tokens.shape[0]
    chunks = length // CHUNK
    empty = pos.shape[0] - NT

    @pl.when(step == 0)
    def _():
        move_heads(load_tile, pos, packed, wri.at[0], load_sems.at[0], 0)
        load_xy(pos, packed, wxy.at[0], wo.at[0], load_sems.at[0], 0, 0, DT)
        zeros[...] = jnp.zeros_like(zeros)
        for t in range(empty):
            pltpu.make_async_copy(zeros.at[t], grads.at[pos[NT + t]], zero_sem).start()

        def one(i, _):
            rows = pl.ds(pl.multiple_of(i * E, E), E)
            x = tokens[rows, :].astype(F32)
            normed_t[:, rows] = (x * norm_rows(x) * gain[...]).T.astype(BF)
            normed_back[rows, :] = jnp.zeros_like(x)
            return 0

        lax.fori_loop(0, length // E, one, 0)
        wait_bytes(zeros, zero_sem)

    wait_xy(wxy.at[slot], wo.at[slot], wri.at[slot], load_sems.at[slot])
    move_heads(load_tile, pos, packed, wri.at[other], load_sems.at[other], after)
    values = params[...]

    for c in range(length // HIGH_ROWS):
        rows = slice(c * HIGH_ROWS, (c + 1) * HIGH_ROWS)
        mixed_back[rows, :] = mm(out_back[rows, :], wo[slot], NT_DIMS)
        half = DT // 2
        load_xy(pos, packed, wxy.at[other], wo.at[other], load_sems.at[other], after, c * half, half)
    row_in = lax.broadcasted_iota(jnp.int32, (CHUNK, BLOCK), 0)

    def fold(v):
        return jnp.sum(v.reshape(CHUNK // 8, 8, BLOCK), axis=0)

    def recur(i, kept):
        keep_after, carry, rec_sum, inp_sum, decay_sum = kept
        rows = pl.ds(pl.multiple_of((chunks - 1 - i) * CHUNK, CHUNK), CHUNK)
        keep = keep_in[rows, :]
        later = jnp.where(row_in == CHUNK - 1, keep_after, pltpu.roll(keep, CHUNK - 1, 0))
        m_back = mixed_back[rows, :]
        bp[rows, BLOCK:] = (m_back * sg_in[rows, :]).astype(BF)
        carried, carry = scan_chunk(later, m_back * g_in[rows, :], carry, True)
        rec_back = carried * p_in[rows, :]
        inp_back = carried * q_in[rows, :]
        conv_back[rows, :] = carried * ga_in[rows, :]
        for h in range(WIDE):
            at = h * 2 * E
            ri[rows, at : at + E] = rec_back[:, h * E : (h + 1) * E].astype(BF)
            ri[rows, at + E : at + 2 * E] = inp_back[:, h * E : (h + 1) * E].astype(BF)
        return (
            keep[0:1],
            carry,
            rec_sum + fold(rec_back),
            inp_sum + fold(inp_back),
            decay_sum + fold(carried * u_in[rows, :]),
        )

    one_row = jnp.zeros((1, BLOCK), F32)
    eight = jnp.zeros((8, BLOCK), F32)
    _, _, rec_sum, inp_sum, decay_sum = lax.fori_loop(
        0, chunks, recur, (one_row, one_row, eight, eight, eight), unroll=2
    )
    small_grad[5:6, :] = jnp.sum(rec_sum, axis=0, keepdims=True)
    small_grad[6:7, :] = jnp.sum(inp_sum, axis=0, keepdims=True)
    small_grad[7:8, :] = jnp.sum(decay_sum, axis=0, keepdims=True) * values[8:9]

    @pl.when(step >= 2)
    def _():
        wait_xy(sxy.at[slot], so.at[slot], sri.at[slot], store_sems.at[slot])

    for h in range(WIDE):
        part = slice(h * 2 * E, (h + 1) * 2 * E)
        one_head = slice(h * E, (h + 1) * E)
        conv_back[:, one_head] += mm(ri[:, part], wri[slot, h], NT_DIMS)
        sri[slot, h] = mm(conv_low[:, one_head], ri[:, part], TN_DIMS).astype(BF)

    def unconvolve(i, sums):
        r = pl.multiple_of(i * CHUNK, CHUNK)
        rows = pl.ds(r, CHUNK)
        back = conv_back[rows, :]
        after_rows = conv_back[pl.ds(pl.multiple_of(jnp.minimum(r + CHUNK, length - 8), 8), 8), :]
        ext = jnp.concatenate([back, jnp.where(i == chunks - 1, 0.0, after_rows)], axis=0)
        now = branch[rows, :]
        total = values[0:1] * back
        out = [sums[0] + fold(back * now)]
        for k in range(1, KW):
            total = total + values[k : k + 1] * ext[k : k + CHUNK]
        bp[rows, :BLOCK] = total.astype(BF)
        before = branch[pl.ds(pl.multiple_of(jnp.maximum(r - 8, 0), 8), 8), :]
        prev = jnp.concatenate([jnp.where(r == 0, 0.0, before), now], axis=0)
        for k in range(1, KW):
            out.append(sums[k] + fold(back * prev[8 - k : 8 - k + CHUNK]))
        out.append(sums[KW] + fold(back))
        return tuple(out)

    sums = lax.fori_loop(0, chunks, unconvolve, (eight,) * (KW + 1), unroll=2)
    for k in range(KW + 1):
        small_grad[k : k + 1, :] = jnp.sum(sums[k], axis=0, keepdims=True)

    for c in range(D // ROWS):
        cols = slice(c * ROWS, (c + 1) * ROWS)
        normed_back[:, cols] += mm(bp[...], wxy[slot, cols, :], NT_DIMS)

    at = step * WIDE
    out_sem = store_sems.at[slot]
    so[slot] = mm(mixed[...], out_back[...], TN_DIMS).astype(BF)
    for c in range(DT):
        move_down(store_tile, pos, grads, so.at[slot], out_sem, AT_OUT + at * DT, c)
    half = D // 2
    for c in range(2):
        rows = slice(c * half, (c + 1) * half)
        sxy[slot, rows, :] = mm(normed_t[rows, :], bp[...]).astype(BF)
        for j in range(DT // 2):
            firsts = (AT_X + at, AT_Y + at)
            move_pair(store_tile, pos, grads, sxy.at[slot], out_sem, firsts, RT, c * (DT // 2) + j)
    move_heads(store_tile, pos, grads, sri.at[slot], out_sem, step)

    @pl.when(step == last)
    def _():
        def fetch(i):
            return pltpu.make_async_copy(
                resid_back.at[pl.ds(i * E, E)], resid_rows.at[i % 2], resid_sems.at[i % 2]
            )

        fetch(0).start()
        gain_sum = jnp.zeros((8, D), F32)
        for i in range(length // E):
            if i + 1 < length // E:
                fetch(i + 1).start()
            fetch(i).wait()
            rows = slice(i * E, (i + 1) * E)
            x = tokens[rows, :].astype(F32)
            n_back = normed_back[rows, :]
            inv = norm_rows(x)
            scaled = n_back * gain[...]
            mean = jnp.mean(scaled * x, axis=-1, keepdims=True)
            x_back = resid_rows[i % 2] + (inv * scaled - x * (inv * inv * inv * mean))
            input_grad[rows, :] = x_back.astype(BF)
            gain_sum = gain_sum + jnp.sum((n_back * x * inv).reshape(E // 8, 8, D), axis=0)
        gain_grad[...] = jnp.sum(gain_sum, axis=0, keepdims=True)
        wait_xy(wxy.at[other], wo.at[other], wri.at[other], load_sems.at[other])
        for s in range(2):
            wait_xy(sxy.at[s], so.at[s], sri.at[s], store_sems.at[s])


def temporal_backward(pos, packed, grads, resid_back, tokens, out_back, gain, params, saved):
    length = tokens.shape[0]
    column = pl.BlockSpec((length, BLOCK), lambda i, *_: (0, i))
    return pl.pallas_call(
        temporal_backward_kernel,
        grid_spec=pltpu.PrefetchScalarGridSpec(
            num_scalar_prefetch=1,
            grid=(R // BLOCK,),
            in_specs=[
                ANY, ANY, ANY,
                whole((length, D)), whole((length, D)), whole((1, D)),
                pl.BlockSpec((16, BLOCK), lambda i, *_: (0, i)),
            ]
            + [column] * 10,
            out_specs=[
                ANY,
                whole((length, D)),
                whole((1, D)),
                pl.BlockSpec((8, BLOCK), lambda i, *_: (0, i)),
            ],
            scratch_shapes=[
                pltpu.VMEM((D, length), BF),
                pltpu.VMEM((length, D), F32),
                pltpu.VMEM((2, D, 2 * BLOCK), BF),
                pltpu.VMEM((2, BLOCK, D), BF),
                pltpu.VMEM((2, WIDE, E, 2 * E), BF),
                pltpu.VMEM((length, 2 * BLOCK), BF),
                pltpu.VMEM((length, 2 * BLOCK), BF),
                pltpu.VMEM((length, BLOCK), F32),
                pltpu.VMEM((length, BLOCK), F32),
                pltpu.VMEM((2, E, D), F32),
                pltpu.VMEM((2, D, 2 * BLOCK), BF),
                pltpu.VMEM((2, BLOCK, D), BF),
                pltpu.VMEM((2, WIDE, E, 2 * E), BF),
                pltpu.VMEM((pos.shape[0] - NT, E, E), BF),
                pltpu.SemaphoreType.DMA((2,)),
                pltpu.SemaphoreType.DMA((2,)),
                pltpu.SemaphoreType.DMA,
                pltpu.SemaphoreType.DMA((2,)),
            ],
        ),
        out_shape=[
            jax.ShapeDtypeStruct(grads.shape, BF),
            jax.ShapeDtypeStruct((length, D), BF),
            jax.ShapeDtypeStruct((1, D), F32),
            jax.ShapeDtypeStruct((8, R), F32),
        ],
        input_output_aliases={2: 0},
        compiler_params=pltpu.CompilerParams(vmem_limit_bytes=60 << 20),
        cost_estimate=pl.CostEstimate(
            flops=12 * length * D * R, bytes_accessed=130 << 20, transcendentals=length * R
        ),
        name="temporal_backward",
    )(pos, packed, grads, resid_back, tokens, out_back, gain, params, *saved)


def lanes_last(src, dst):
    count, lanes = src.shape[0], dst.shape[2]

    def one(q, _):
        at = pl.multiple_of(q * 8, 8)
        part = jnp.swapaxes(src[:, pl.ds(at, 8), :], 0, 1)
        if count < lanes:
            part = jnp.concatenate([part, jnp.zeros((8, lanes - count, E), F32)], axis=1)
        for k in range(8):
            dst[at + k] = part[k].T
        return 0

    lax.fori_loop(0, src.shape[1] // 8, one, 0)


def lanes_first(src, dst):
    count = dst.shape[0]

    def one(q, _):
        at = pl.multiple_of(q * 8, 8)
        part = jnp.swapaxes(src[:, pl.ds(at, 8), :], 0, 1)
        turned = jnp.stack([part[i].T[:count] for i in range(8)], axis=0)
        dst[:, pl.ds(at, 8), :] = jnp.swapaxes(turned, 0, 1)
        return 0

    lax.fori_loop(0, src.shape[1] // 8, one, 0)


def solve_kernel(gram, rows, left, right, factor, solved, inverse):
    size, tall = gram.shape[1], 32
    lanes_last(gram, factor)

    def eliminate(ref, acc, r0, count, j0, begin):
        window = pl.ds(r0, count)

        def one(k, acc):
            col = ref[k, window, :]
            return tuple(
                acc[c] - col * factor[k, j0 + c : j0 + c + 1, :] for c in range(8)
            )

        def eight(q, acc):
            for u in range(8):
                acc = one(q * 8 + u, acc)
            return acc

        return lax.fori_loop(begin // 8, j0 // 8, eight, acc)

    def finish(ref, acc, r0, count, j0, scales):
        acc = list(acc)
        for c in range(8):
            for c2 in range(c):
                acc[c] = acc[c] - acc[c2] * factor[j0 + c2, j0 + c : j0 + c + 1, :]
            acc[c] = acc[c] * scales[c]
            ref[j0 + c, pl.ds(r0, count), :] = acc[c]

    for j0 in range(0, size, 8):
        acc = tuple(factor[j0 + c, j0 : j0 + 8, :] for c in range(8))
        cols = list(eliminate(factor, acc, j0, 8, j0, 0))
        scales = []
        for c in range(8):
            pivot = cols[c][c : c + 1]
            scale = lax.rsqrt(pivot)
            scale = scale * (1.5 - 0.5 * (pivot * scale) * scale)
            scales.append(scale)
            cols[c] = cols[c] * scale
            for c2 in range(c + 1, 8):
                cols[c2] = cols[c2] - cols[c] * cols[c][c2 : c2 + 1]
        for c in range(8):
            factor[j0 + c, j0 : j0 + 8, :] = cols[c]
        at = j0 + 8
        while at < size:
            count = min(tall, size - at)
            acc = tuple(factor[j0 + c, at : at + count, :] for c in range(8))
            acc = eliminate(factor, acc, at, count, j0, 0)
            finish(factor, acc, at, count, j0, scales)
            at += count
        for at in range(0, size, tall):
            if at > j0:
                for c in range(8):
                    solved[j0 + c, at : at + tall, :] = jnp.zeros((tall, solved.shape[2]), F32)
                continue
            row = lax.broadcasted_iota(jnp.int32, (tall, solved.shape[2]), 0) + at
            acc = tuple(jnp.where(row == j0 + c, 1.0, 0.0) for c in range(8))
            acc = eliminate(solved, acc, at, tall, j0, at)
            finish(solved, acc, at, tall, j0, scales)

    lanes_first(solved, inverse)
    slots = left.shape[0]

    def one(m, _):
        for side, out in enumerate((left, right)):
            at = side * slots + m
            out[m] = product(split3(rows[at]), split3(inverse[at]), NN, 3)
        return 0

    lax.fori_loop(0, slots, one, 0, unroll=2 if slots % 2 == 0 else 1)


def solve(gram, rows):
    count = gram.shape[0]
    spare = -count % 8
    if spare:
        gram = jnp.pad(gram, ((0, spare), (0, 0), (0, 0)))
    lanes = E * -(-count // E)
    vmem = pl.BlockSpec(memory_space=pltpu.VMEM)
    shape = jax.ShapeDtypeStruct((count // 2, E, E), F32)
    return pl.pallas_call(
        solve_kernel,
        out_shape=[shape, shape],
        in_specs=[vmem, vmem],
        out_specs=[vmem, vmem],
        scratch_shapes=[
            pltpu.VMEM((E, E, lanes), F32),
            pltpu.VMEM((E, E, lanes), F32),
            pltpu.VMEM(gram.shape, F32),
        ],
        compiler_params=pltpu.CompilerParams(vmem_limit_bytes=56 << 20),
        cost_estimate=pl.CostEstimate(
            flops=60 * 10**9, bytes_accessed=12 * gram.size, transcendentals=0
        ),
        name="cholesky_solve",
    )(gram, rows)


def split3(x):
    one = x.astype(BF)
    rest = x - one.astype(F32)
    two = rest.astype(BF)
    return one, two, (rest - two.astype(F32)).astype(BF)


def product(left, right, dims, terms):
    pairs = [(a, t - a) for t in range(terms - 1, -1, -1) for a in range(t + 1)]
    pairs = [(a, b) for a, b in pairs if a < len(left) and b < len(right)]
    (left_axis,), (right_axis,) = dims[0]
    return mm(
        jnp.concatenate([left[a] for a, _ in pairs], axis=left_axis),
        jnp.concatenate([right[b] for _, b in pairs], axis=right_axis),
        dims,
    )


def rotate_kernel(
    own, weights, first, second, left, right, left_stat, right_stat, *refs
):
    weight_new, first_new, second_new, left_stat_new, right_stat_new, gram, rows = refs[-7:]
    each = range(own.shape[0])
    grads = [split3(own[i])[:2] for i in each]
    lefts = [split3(left[i]) for i in each]
    rights = [split3(right[i]) for i in each]
    sides = (
        (left_stat, left_stat_new, lefts, NT_DIMS),
        (right_stat, right_stat_new, rights, TN_DIMS),
    )
    halves = [split3(product(lefts[i][:2], grads[i], TN_DIMS, 2))[:2] for i in each]
    squares = [[product(grads[i], grads[i], side[3], 2) for i in each] for side in sides]
    turned = [product(halves[i], rights[i][:2], NN, 2) for i in each]
    moved = [[None for i in each] for side in sides]
    for s, (stat, stat_new, basis, _) in enumerate(sides):
        for i in each:
            now = BETA_STAT * stat[i] + (1.0 - BETA_STAT) * squares[s][i]
            stat_new[i] = now
            moved[s][i] = product(split3(now), basis[i], NN, 3)
            rows[s, i] = moved[s][i]
    scaled = []
    for i in each:
        first_now = BETA_ONE * first[i] + (1.0 - BETA_ONE) * turned[i]
        second_now = BETA_TWO * second[i] + (1.0 - BETA_TWO) * turned[i] * turned[i]
        first_new[i] = first_now
        second_new[i] = second_now
        scaled.append(
            first_now
            / (1.0 - BETA_ONE**STEP)
            / (jnp.sqrt(second_now / (1.0 - BETA_TWO**STEP)) + ADAM_EPS)
        )
    back = [split3(product(lefts[i][:2], split3(scaled[i])[:2], NN, 2))[:2] for i in each]
    for s in range(2):
        for i in each:
            pieces = split3(moved[s][i])
            gram[s, i] = product(pieces, pieces, TN_DIMS, 3)
    for i in each:
        update = product(back[i], rights[i][:2], NT_DIMS, 2)
        weight_new[i] = weights[i] - RATE * (update + DECAY * weights[i])


def rotate(own, spans, states, before):
    slots = states[0].shape[0]
    count = sum(n for _, n in spans)
    group = max(g for g in (1, 2, 4) if all(b % g == 0 and n % g == 0 for b, n in spans))
    begin, size = spans[0][0] // group, spans[0][1] // group
    other = spans[-1][0] // group - size if len(spans) > 1 else begin

    def place(i):
        return (jnp.where(i < size, i + begin, i + other), 0, 0)

    block = pl.BlockSpec((group, E, E), place)
    pair = pl.BlockSpec((2, group, E, E), lambda i: (0, *place(i)))
    one = jax.ShapeDtypeStruct((slots, E, E), F32)
    two = jax.ShapeDtypeStruct((2, slots, E, E), F32)
    return pl.pallas_call(
        rotate_kernel,
        grid=(count // group,),
        in_specs=[pl.BlockSpec((group, E, E), lambda i: (i, 0, 0))] + [block] * 7 + [ANY] * len(before),
        out_specs=[block] * 5 + [pair] * 2,
        out_shape=[one] * 5 + [two] * 2,
        input_output_aliases={8 + i: i for i in range(len(before))},
        compiler_params=pltpu.CompilerParams(vmem_limit_bytes=50 << 20),
        cost_estimate=pl.CostEstimate(
            flops=count * 10**9, bytes_accessed=16 * 4 * count * E * E, transcendentals=0
        ),
        name="rotate",
    )(own, *states, *before)


def small_step(grads, weights, first_vals, second_vals):
    first_new = BETA_ONE * first_vals + (1.0 - BETA_ONE) * grads
    second_new = BETA_TWO * second_vals + (1.0 - BETA_TWO) * grads * grads
    scaled = (
        first_new
        / (1.0 - BETA_ONE**STEP)
        / (jnp.sqrt(second_new / (1.0 - BETA_TWO**STEP)) + ADAM_EPS)
    )
    return (weights - SMALL_RATE * scaled, first_new, second_new)


def small_tile(small):
    lead = small.shape[:-1]
    pad = [(0, 0)] * len(lead) + [(0, E * E - small.shape[-1])]
    return jnp.pad(small, pad).reshape(*lead, E, E)


def swap_pairs(size, bit):
    return [(i, i ^ bit) for i in range(size)]


def split_bits(chips):
    bits = [1 << b for b in range(chips.bit_length() - 1)]
    return bits[: len(bits) // 2], bits[len(bits) // 2 :]


def part_sizes(per_device):
    first = max(1, round(per_device / 15)) * 4
    second = 2 * first
    return [first, second], per_device - first - second


def block_of(along, across, size, other, half):
    edge = jnp.where(
        (across == 0) & (along > 0), 2 * along if half == 0 else 2 * (other - 1 + along), 0
    )
    edge = jnp.where(
        (across > 0) & (along == 0),
        2 * (size - 1 + across) if half == 0 else 2 * across,
        edge,
    )
    inner = 2 * (size + other - 1) + half * (size - 1) * (other - 1)
    inner = inner + (across - 1) * (size - 1) + along - 1
    return jnp.where((across > 0) & (along > 0), inner, edge + half)


def place_of_tile(holder, inner, per_device, chips, cores, owners):
    z, core, chip = holder % owners, holder // owners % cores, holder // (owners * cores)
    low, high = split_bits(chips)
    width, height = 1 << len(low), 1 << len(high)
    far = chip ^ lax.axis_index("yx")
    x, y = far % width, far // width
    far_core = core ^ lax.axis_index("core")
    far_z = (z - lax.axis_index("owner")) % owners
    sizes, rest = part_sizes(per_device)
    total, at = jnp.zeros_like(inner), 0
    for size in sizes:
        side = size // 2
        for half in range(2):
            args = (x, y, width, height, 0) if half == 0 else (y, x, height, width, 1)
            block = far_core * (2 * chips) + block_of(*args)
            place = at * chips * cores * owners + (block * owners + far_z) * side
            begin = at + half * side
            here = (inner >= begin) & (inner < begin + side)
            total = jnp.where(here, place + inner - begin, total)
        at += size
    place = at * chips * cores * owners + ((far_core * owners + far_z) * chips + far) * rest
    return jnp.where(inner >= at, place + inner - at, total)


def add_low(a, b):
    return (a.astype(F32) + b.astype(F32)).astype(BF)


def to_core(x):
    return lax.ppermute(x, "core", [(0, 1), (1, 0)])


def to_chip(x, chips, bit):
    return lax.ppermute(x, "yx", swap_pairs(chips, bit))


RIGHT = [(0, 1), (1, 2), (2, 3)]
LEFT = [(1, 0), (2, 1), (3, 2)]


def hop_one(x):
    return lax.ppermute(x, "owner", LEFT), lax.ppermute(x, "owner", RIGHT)


def hop_two(near, z):
    from_right = lax.ppermute(near[0], "owner", LEFT[:2])
    from_left = lax.ppermute(near[1], "owner", RIGHT[1:])
    return jnp.where(z < 2, from_right, from_left)


def hop_three(middle):
    return lax.ppermute(middle, "owner", [(1, 0), (2, 3)])


def line_join(x, near, middle, ends, z):
    return [x, jnp.where(z == 3, ends, near[0]), middle, jnp.where(z == 0, ends, near[1])]


def halves_first(blocks):
    side = blocks[0].shape[0] // 2
    return jnp.concatenate([b[:side] for b in blocks] + [b[side:] for b in blocks], axis=0)


def butterfly(x, bits, chips):
    pieces = [x]
    for bit in bits:
        pieces = pieces + [to_chip(p, chips, bit) for p in pieces]
    return pieces[1:]


def tie(*trees):
    return lax.optimization_barrier(trees)


def spread_chunk(joined, low, high, chips):
    half = joined.shape[0] // 2
    along_x = butterfly(joined, low, chips)
    along_y = butterfly(joined, high, chips)
    return along_x, along_y, half


def spread_rest(along_x, along_y, half, low, high, chips):
    inner = []
    for p in along_y:
        inner += butterfly(p[:half], low, chips)
    for p in along_x:
        inner += butterfly(p[half:], high, chips)
    return inner


def put(buffer, pieces, at):
    for piece in pieces:
        buffer = lax.dynamic_update_slice(buffer, piece, (at, 0, 0))
        at += piece.shape[0]
    return buffer


def gather_tiles(mine, chips, devices, beside):
    z = lax.axis_index("owner")
    low, high = split_bits(chips)
    per_device = mine.shape[0]
    (first, second), rest = part_sizes(per_device)
    one, two, three = mine[:first], mine[first : first + second], mine[first + second :]
    buffer = blank(devices * per_device)

    def join(x, near, middle, ends):
        return halves_first(line_join(x, near, middle, ends, z))

    near = hop_one(one)
    three = jnp.concatenate([three] + butterfly(three, low + high, chips), axis=0)
    middle = hop_two(near, z)
    middle, three = tie(middle, three)
    one = join(one, near, middle, hop_three(middle))
    one, two = tie(one, two)

    along_x, along_y, half = spread_chunk(one, low, high, chips)
    near = hop_one(two)
    middle = hop_two(near, z)
    along_x, along_y, middle = tie(along_x, along_y, middle)
    inner = spread_rest(along_x, along_y, half, low, high, chips)
    two = join(two, near, middle, hop_three(middle))
    pieces_one = [one] + along_x + along_y + inner
    two, pieces_one, three, beside = tie(two, pieces_one, three, beside)

    along_x, along_y, half = spread_chunk(two, low, high, chips)
    near = hop_one(three)
    middle = hop_two(near, z)
    joined = jnp.concatenate(pieces_one, axis=0)
    along_x, along_y, middle, joined = tie(along_x, along_y, middle, joined)
    inner = spread_rest(along_x, along_y, half, low, high, chips)
    ends = hop_three(middle)
    far_one = to_core(joined)
    edge = [two] + along_x + along_y
    buffer = put(buffer, [joined], 0)
    buffer = put(buffer, edge, first * devices)
    inner, ends, edge, beside, buffer = tie(inner, ends, edge, beside, buffer)

    beside = lax.all_to_all(beside, AXES, split_axis=0, concat_axis=0, tiled=True)
    pieces_three = line_join(three, near, middle, ends, z)
    far_two = [to_core(p) for p in edge + inner]
    far_even = to_core(jnp.concatenate(pieces_three[::2], axis=0))
    far_odd = to_core(jnp.concatenate(pieces_three[1::2], axis=0))
    size = three.shape[0]
    far_three = [far_even[:size], far_odd[:size], far_even[size:], far_odd[size:]]
    buffer = put(buffer, [far_one], joined.shape[0])
    at = first * devices + sum(p.shape[0] for p in edge)
    buffer = put(buffer, inner + far_two, at)
    return put(buffer, pieces_three + far_three, (first + second) * devices), beside


def fold_butterfly(blocks, bits, chips):
    for bit in bits[::-1]:
        far = [to_chip(b, chips, bit) for b in blocks[len(blocks) // 2 :]]
        blocks = [add_low(a, b) for a, b in zip(blocks, far)]
    return blocks[0]


def fold_one(x, z):
    x = x.reshape(4, -1, E, E)
    far = lax.ppermute(jnp.where(z == 0, x[3], x[1]), "owner", [(0, 1), (3, 2)])
    return x, add_low(x[2], far)


def fold_two(state):
    x, middle = state
    from_left = lax.ppermute(middle, "owner", RIGHT[:2])
    from_right = lax.ppermute(middle, "owner", LEFT[1:])
    return x[0], add_low(x[1], from_left), add_low(x[3], from_right)


def fold_three(state, last):
    mine, right, left = state
    from_left = lax.ppermute(right, "owner", RIGHT)
    from_right = lax.ppermute(left, "owner", LEFT)
    total = mine.astype(F32) + from_left.astype(F32) + from_right.astype(F32)
    return total if last else total.astype(BF)


def edge_blocks(chips, low, high):
    return 2 * ((1 << len(low)) + (1 << len(high)) - 1)


def fold_inner(edge, inner, low, high, chips):
    width, height = 1 << len(low), 1 << len(high)
    half = edge.shape[0] // edge_blocks(chips, low, high)
    edge, inner = edge.reshape(-1, half, E, E), inner.reshape(-1, half, E, E)
    along_x = [edge[2 * i : 2 * i + 2] for i in range(width)]
    along_y = [edge[2 * (width - 1 + i) : 2 * (width - 1 + i) + 2] for i in range(1, height)]
    for i in range(1, height):
        begin = (i - 1) * (width - 1)
        old = along_y[i - 1]
        blocks = [old[0]] + [inner[begin + j] for j in range(width - 1)]
        along_y[i - 1] = jnp.stack([fold_butterfly(blocks, low, chips), old[1]])
    for i in range(1, width):
        begin = (width - 1) * (height - 1) + (i - 1) * (height - 1)
        blocks = [along_x[i][1]] + [inner[begin + j] for j in range(height - 1)]
        along_x[i] = jnp.stack([along_x[i][0], fold_butterfly(blocks, high, chips)])
    return along_x[0], along_x[1:], along_y


def fold_outer(state, low, high, chips, owners):
    own, along_x, along_y = state
    zero = jnp.zeros_like(own)
    from_x = fold_butterfly([zero] + along_x, low, chips)
    from_y = fold_butterfly([zero] + along_y, high, chips)
    x = own.astype(F32) + from_x.astype(F32) + from_y.astype(F32)
    x = x.astype(BF).reshape(2, owners, -1, E, E)
    return x.transpose(1, 0, 2, 3, 4).reshape(-1, E, E)


def scatter_tiles(grads, chips, devices, owners):
    z = lax.axis_index("owner")
    low, high = split_bits(chips)
    per_device = grads.shape[0] // devices
    (first, second), rest = part_sizes(per_device)

    def cut(begin, size):
        halfway = size * devices // 2
        edge = halfway // (2 * chips) * edge_blocks(chips, low, high)
        at = begin * devices
        cuts = [at, at + edge, at + halfway, at + halfway + edge, at + 2 * halfway]
        return [grads[a:b] for a, b in zip(cuts, cuts[1:])]

    one, two = cut(0, first), cut(first, second)
    three = grads[(first + second) * devices :].reshape(2, -1, E, E)

    got_inner = to_core(two[3])
    got_inner, far = tie(got_inner, two[2])
    got_edge = to_core(far)
    got_edge, far_one, far_three = tie(got_edge, one[2:], three[1])
    got_three, got_one = to_core(far_three), [to_core(x) for x in far_one]
    two_inner = add_low(two[1], got_inner)
    two = fold_inner(add_low(two[0], got_edge), two_inner, low, high, chips)
    three = fold_one(add_low(three[0], got_three), z)
    two, got_one = tie(two, got_one)

    two = fold_outer(two, low, high, chips, owners)
    three = fold_two(three)
    three = fold_three(three, False)
    two, three = tie(two, three)

    one = [add_low(a, b) for a, b in zip(one, got_one)]
    one = fold_inner(one[0], one[1], low, high, chips)
    two = fold_one(two, z)
    two = fold_two(two)
    one = fold_outer(one, low, high, chips, owners)
    two = fold_three(two, True)
    one, two = tie(one, two)

    blocks = list(three.reshape(chips, -1, E, E))
    bits = low + high
    for bit in bits[::-1]:
        moved = [to_chip(b, chips, bit) for b in blocks[len(blocks) // 2 :]]
        blocks = [
            a.astype(F32) + b.astype(F32) if bit == bits[0] else add_low(a, b)
            for a, b in zip(blocks, moved)
        ]
    one = fold_three(fold_two(fold_one(one, z)), True)
    return two, jnp.concatenate([one, blocks[0]], axis=0)


def blank_kernel(out):
    pass


def blank(count):
    return pl.pallas_call(
        blank_kernel,
        out_shape=jax.ShapeDtypeStruct((count, E, E), BF),
        out_specs=ANY,
        name="blank",
    )()


def body(
    inputs,
    cotangent,
    lengths,
    balance,
    owner_slot_tile,
    master,
    first_moment,
    second_moment,
    left_basis,
    right_basis,
    left_stat,
    right_stat,
    small_master,
    small_first,
    small_second,
):
    yx, cores, owners = (lax.axis_size(name) for name in AXES)
    devices = yx * cores * owners
    rank = lax.axis_index(AXES)
    tokens = inputs[0]
    seq_len = tokens.shape[0]
    held = master.shape[0]
    small_held = small_master.shape[0]
    per_device = held + 1

    place_args = (per_device, yx, cores, owners)

    slots = jnp.arange(owner_slot_tile.shape[0], dtype=jnp.int32)
    place = place_of_tile(slots // held, slots % held, *place_args)
    hit = owner_slot_tile[:, None] == slots[None, :]
    pos = jnp.sum(jnp.where(hit, place[:, None], 0), axis=0)
    ranks = jnp.arange(devices, dtype=jnp.int32)
    small_place = place_of_tile(ranks, jnp.full_like(ranks, held), *place_args)

    mine = jnp.concatenate([master.astype(BF), small_tile(small_master.astype(BF))[None]], axis=0)
    shares = cotangent.reshape(devices, seq_len // devices, D)
    mine, pos = tie(mine, pos)
    packed, spread = gather_tiles(mine, yx, devices, shares)

    used = -(-small_held // E)
    small = packed[:, :used][small_place].reshape(devices, used * E)[:, :small_held]
    small = small.reshape(-1).astype(F32)
    gain_one, gain_two = small[None, :D], small[None, D : 2 * D]
    wide = small[2 * D :].reshape(KW + 4, R)
    decay_log = wide[KW + 3]
    params = jnp.concatenate(
        [
            wide[: KW + 3],
            -8.0 * jax.nn.softplus(-decay_log)[None],
            8.0 * jax.nn.sigmoid(-decay_log)[None],
            jnp.zeros((16 - KW - 5, R), F32),
        ],
        axis=0,
    )

    place_of = jnp.sum(
        jnp.where(
            balance[:, None] == jnp.arange(devices, dtype=jnp.int32)[None, :],
            jnp.arange(devices, dtype=jnp.int32)[:, None],
            0,
        ),
        axis=0,
    )
    params, spread = tie(params, spread)
    back = lax.all_to_all(spread[place_of], AXES, split_axis=0, concat_axis=0, tiled=True)
    live = jnp.arange(seq_len, dtype=jnp.int32) < lengths[rank]
    back = jnp.where(live[:, None], back.reshape(seq_len, D), 0).astype(BF)

    saved, resid = temporal_forward(pos, packed, tokens, gain_one, params)
    grads, activation, resid_back, out_back, grad_gain_two = ffn(pos, packed, resid, back, gain_two)
    grads, input_grad, grad_gain_one, small_grad = temporal_backward(
        pos, packed, grads, resid_back, tokens, out_back, gain_one, params, saved
    )

    small_grads = jnp.concatenate(
        [grad_gain_one.reshape(-1), grad_gain_two.reshape(-1), small_grad.reshape(-1)], axis=0
    )
    small_tiles = small_tile(small_grads.reshape(devices, small_held)).astype(BF)
    grads = grads.at[small_place].set(small_tiles)
    own_two, own_one = scatter_tiles(grads, yx, devices, owners)
    own_small = own_one[-1].reshape(-1)[:small_held]

    (first, second), _ = part_sizes(per_device)
    states = (
        master, first_moment, second_moment, left_basis, right_basis, left_stat, right_stat
    )
    spans_two = [(first, second)]
    spans_one = [(0, first), (first + second, held - first - second)]
    news = rotate(own_two, spans_two, states, ())
    *news, gram, rows = rotate(own_one, spans_one, states, news)
    new_left, new_right = solve(gram.reshape(-1, E, E), rows.reshape(-1, E, E))
    new_master, new_first, new_second, new_left_stat, new_right_stat = news

    small_new, small_first_new, small_second_new = small_step(
        own_small, small_master, small_first, small_second
    )
    return (
        activation[None],
        input_grad[None],
        new_master,
        new_first,
        new_second,
        new_left,
        new_right,
        new_left_stat,
        new_right_stat,
        small_new,
        small_first_new,
        small_second_new,
    )


def solution(mesh):
    dp, owner = mesh.devices.shape
    fine = Mesh(mesh.devices.reshape(dp // 2, 2, owner), AXES)
    cut = P(AXES)
    return jax.shard_map(
        body,
        mesh=fine,
        in_specs=(cut, cut, P(), P(), P()) + (cut,) * 10,
        out_specs=(cut,) * 12,
        check_vma=False,
    )
```

```python
import functools
import math

import jax
import jax.numpy as jnp
from jax import lax
from jax.experimental import pallas as pl
from jax.experimental.pallas import tpu as pltpu
from jax.sharding import Mesh
from jax.sharding import PartitionSpec as P

D = 1536
R = 2048
F = 4608
KW = 4
STEP = 5
NT = 1904
E = 128

EPS = 1e-06
BETA_ONE = 0.5
BETA_TWO = 0.6
BETA_STAT = 0.5
RATE = 0.02
SMALL_RATE = 0.6
DECAY = 0.01
ADAM_EPS = 1e-08
HIGH = lax.Precision.HIGHEST

DT, RT, FT = D // E, R // E, F // E
AT_X = 0
AT_Y = DT * RT
AT_OUT = 2 * DT * RT
AT_REC = 3 * DT * RT
AT_INP = AT_REC + RT
AT_GATE = AT_INP + RT
AT_UP = AT_GATE + DT * FT
AT_DOWN = AT_UP + DT * FT

AXES = ("yx", "core", "owner")
BLOCK = 256
WIDE = BLOCK // E
FFN_BLOCK = 256
FFN_WIDE = FFN_BLOCK // E
CHUNK = 16
ROWS = 256
HIGH_ROWS = 512

BF = jnp.bfloat16
F32 = jnp.float32

NN = (((1,), (0,)), ((), ()))
NT_DIMS = (((1,), (1,)), ((), ()))
TN_DIMS = (((0,), (0,)), ((), ()))


def mm(left, right, dims=NN):
    return lax.dot_general(left, right, dims, preferred_element_type=F32)


def gelu_pair(x):
    c = math.sqrt(2.0 / math.pi)
    sq = x * x
    t = jnp.tanh(x * (c + (c * 0.044715) * sq))
    half = 0.5 + 0.5 * t
    slope = half + (0.5 * x) * (1.0 - t * t) * (c + (3.0 * c * 0.044715) * sq)
    return x * half, slope


def gelu_only(x):
    c = math.sqrt(2.0 / math.pi)
    return x * (0.5 + 0.5 * jnp.tanh(x * (c + (c * 0.044715) * (x * x))))


def minus_expm1(y, exp_y):
    poly = 1.0 + y * (1.0 / 7.0)
    for n in (6.0, 5.0, 4.0, 3.0, 2.0):
        poly = 1.0 + (y * (1.0 / n)) * poly
    return jnp.where(y > -0.35, -y * poly, 1.0 - exp_y)


def whole(shape):
    return pl.BlockSpec(shape, lambda *_: (0,) * len(shape), pipeline_mode=pl.Buffered(1))


ANY = pl.BlockSpec(memory_space=pl.ANY)


def wait_bytes(ref, sem):
    pltpu.make_async_copy(ref, ref, sem).wait()


def load_tile(pos, packed, tile, dst, row, col, sem):
    pltpu.make_async_copy(
        packed.at[pos[tile]], dst.at[pl.ds(row * E, E), pl.ds(col * E, E)], sem
    ).start()


def store_tile(pos, packed, tile, src, row, col, sem):
    pltpu.make_async_copy(
        src.at[pl.ds(row * E, E), pl.ds(col * E, E)], packed.at[pos[tile]], sem
    ).start()


def move_pair(move, pos, packed, ref, sem, firsts, across, row, wide=WIDE):
    for m, first in enumerate(firsts):
        for c in range(wide):
            move(pos, packed, first + row * across + c, ref, row, m * wide + c, sem)


def move_down(move, pos, packed, ref, sem, first, col, wide=WIDE):
    for r in range(wide):
        move(pos, packed, first + r * DT + col, ref, r, col, sem)


def move_heads(move, pos, packed, ref, sem, step):
    for h in range(WIDE):
        for base, col in ((AT_REC, 0), (AT_INP, 1)):
            move(pos, packed, base + step * WIDE + h, ref.at[h], 0, col, sem)


def load_xy(pos, packed, wxy, wo, sem, step, begin, count):
    at = step * WIDE
    for i in range(count):
        move_pair(load_tile, pos, packed, wxy, sem, (AT_X + at, AT_Y + at), RT, begin + i)
        move_down(load_tile, pos, packed, wo, sem, AT_OUT + at * DT, begin + i)


def wait_xy(wxy, wo, wri, sem):
    wait_bytes(wxy, sem)
    wait_bytes(wo, sem)
    wait_bytes(wri, sem)


def conv_chunk(ref, r, taps, bias):
    now = ref[pl.ds(r, CHUNK), :]
    before = ref[pl.ds(pl.multiple_of(jnp.maximum(r - 8, 0), 8), 8), :]
    ext = jnp.concatenate([jnp.where(r == 0, 0.0, before), now], axis=0)
    total = bias + taps[0:1] * now
    for k in range(1, KW):
        total = total + taps[k : k + 1] * ext[8 - k : 8 - k + CHUNK]
    return total


def heads_of(pre, part):
    return jnp.concatenate(
        [pre[:, h * 2 * E + part * E : h * 2 * E + (part + 1) * E] for h in range(WIDE)], axis=1
    )


def scan_chunk(a, b, carry, reverse):
    groups = CHUNK // 8
    shape = (groups, 8, a.shape[-1])
    a, b = a.reshape(shape), b.reshape(shape)
    row = lax.broadcasted_iota(jnp.int32, shape, 1)
    for d in (1, 2, 4):
        turn = 8 - d if reverse else d
        ok = row < 8 - d if reverse else row >= d
        a_far = pltpu.roll(a, turn, 1)
        b_far = pltpu.roll(b, turn, 1)
        b = b + a * jnp.where(ok, b_far, 0.0)
        a = a * jnp.where(ok, a_far, 1.0)
    out = [None] * groups
    for g in range(groups)[:: -1 if reverse else 1]:
        out[g] = b[g] + a[g] * carry
        carry = out[g][0:1] if reverse else out[g][7:8]
    return jnp.concatenate(out, axis=0), carry


def norm_rows(x):
    return lax.rsqrt(jnp.mean(x * x, axis=-1, keepdims=True) + EPS)


def temporal_forward_kernel(
    pos, packed, tokens, gain, params,
    branch, keep_out, u_out, p_out, q_out, ga_out, g_out, sg_out, conv_low, mixed, resid,
    normed, wxy, wo, wri, gate_pre, pre, sems,
):
    step = pl.program_id(0)
    last = pl.num_programs(0) - 1
    slot = lax.rem(step, 2)
    other = 1 - slot
    after = jnp.minimum(step + 1, last)
    length = tokens.shape[0]

    @pl.when(step == 0)
    def _():
        move_heads(load_tile, pos, packed, wri.at[0], sems.at[0], 0)
        load_xy(pos, packed, wxy.at[0], wo.at[0], sems.at[0], 0, 0, DT)

        def one(i, _):
            rows = pl.ds(pl.multiple_of(i * E, E), E)
            x = tokens[rows, :].astype(F32)
            normed[rows, :] = (x * norm_rows(x) * gain[...]).astype(BF)
            resid[rows, :] = x
            return 0

        lax.fori_loop(0, length // E, one, 0)

    wait_xy(wxy.at[slot], wo.at[slot], wri.at[slot], sems.at[slot])
    move_heads(load_tile, pos, packed, wri.at[other], sems.at[other], after)

    for c in range(length // HIGH_ROWS):
        rows = slice(c * HIGH_ROWS, (c + 1) * HIGH_ROWS)
        both = mm(normed[rows, :], wxy[slot])
        branch[rows, :] = both[:, :BLOCK]
        gate_pre[rows, :] = both[:, BLOCK:]
        half = DT // 2
        load_xy(pos, packed, wxy.at[other], wo.at[other], sems.at[other], after, c * half, half)
    values = params[...]

    def convolve(i, _):
        r = pl.multiple_of(i * CHUNK, CHUNK)
        conv_low[pl.ds(r, CHUNK), :] = conv_chunk(branch, r, values[0:4], values[4:5]).astype(BF)
        return 0

    lax.fori_loop(0, length // CHUNK, convolve, 0, unroll=4)
    for h in range(WIDE):
        pre[:, h * 2 * E : (h + 1) * 2 * E] = mm(conv_low[:, h * E : (h + 1) * E], wri[slot, h])

    row_in = lax.broadcasted_iota(jnp.int32, (CHUNK, BLOCK), 0)

    def recur(i, carry):
        rows = pl.ds(pl.multiple_of(i * CHUNK, CHUNK), CHUNK)
        recall = jax.nn.sigmoid(heads_of(pre[rows, :], 0) + values[5:6])
        admit = jax.nn.sigmoid(heads_of(pre[rows, :], 1) + values[6:7])
        log_keep = recall * values[7:8]
        keep = jnp.exp(log_keep)
        keep_sq = keep * keep
        gap = jnp.sqrt(minus_expm1(2.0 * log_keep, keep_sq))
        conv = conv_low[rows, :].astype(F32)
        ga = gap * admit
        driven = ga * conv
        state, carry_out = scan_chunk(keep, driven, carry, False)
        prior = jnp.where(row_in == 0, carry, pltpu.roll(state, 1, 0))
        g, slope = gelu_pair(gate_pre[rows, :])
        mixed[rows, :] = (state * g).astype(BF)
        g_out[rows, :] = g
        sg_out[rows, :] = state * slope
        keep_out[rows, :] = keep
        ga_out[rows, :] = ga
        q_out[rows, :] = driven * (1.0 - admit)
        u = (prior * keep - (admit * conv) * (keep_sq / gap)) * recall
        u_out[rows, :] = u
        p_out[rows, :] = u * ((1.0 - recall) * values[7:8])
        return carry_out

    lax.fori_loop(0, length // CHUNK, recur, jnp.zeros((1, BLOCK), F32), unroll=4)

    for c in range(D // ROWS):
        cols = slice(c * ROWS, (c + 1) * ROWS)
        resid[:, cols] += mm(mixed[...], wo[slot, :, cols])

    @pl.when(step == last)
    def _():
        wait_xy(wxy.at[other], wo.at[other], wri.at[other], sems.at[other])


def temporal_forward(pos, packed, tokens, gain, params):
    length = tokens.shape[0]
    column = pl.BlockSpec((length, BLOCK), lambda i, *_: (0, i))
    wide = jax.ShapeDtypeStruct((length, R), F32)
    low = jax.ShapeDtypeStruct((length, R), BF)
    *saved, resid = pl.pallas_call(
        temporal_forward_kernel,
        grid_spec=pltpu.PrefetchScalarGridSpec(
            num_scalar_prefetch=1,
            grid=(R // BLOCK,),
            in_specs=[
                ANY,
                whole((length, D)),
                whole((1, D)),
                pl.BlockSpec((16, BLOCK), lambda i, *_: (0, i)),
            ],
            out_specs=[column] * 10 + [whole((length, D))],
            scratch_shapes=[
                pltpu.VMEM((length, D), BF),
                pltpu.VMEM((2, D, 2 * BLOCK), BF),
                pltpu.VMEM((2, BLOCK, D), BF),
                pltpu.VMEM((2, WIDE, E, 2 * E), BF),
                pltpu.VMEM((length, BLOCK), F32),
                pltpu.VMEM((length, 2 * BLOCK), F32),
                pltpu.SemaphoreType.DMA((2,)),
            ],
        ),
        out_shape=[wide] * 8 + [low] * 2 + [jax.ShapeDtypeStruct((length, D), F32)],
        compiler_params=pltpu.CompilerParams(vmem_limit_bytes=56 << 20),
        cost_estimate=pl.CostEstimate(
            flops=2 * length * D * R * 3, bytes_accessed=110 << 20, transcendentals=6 * length * R
        ),
        name="temporal_forward",
    )(pos, packed, tokens, gain, params)
    return saved, resid


def load_ffn(pos, packed, wgu, wd, sem, step, begin, count):
    at = step * FFN_WIDE
    for i in range(count):
        move_pair(load_tile, pos, packed, wgu, sem, (AT_GATE + at, AT_UP + at), FT, begin + i, FFN_WIDE)
        move_down(load_tile, pos, packed, wd, sem, AT_DOWN + at * DT, begin + i, FFN_WIDE)


def ffn_kernel(
    pos, packed, resid, back, gain, grads, activation, resid_back, out_back, gain_grad,
    normed, normed_t, total, normed_back, wgu, wd, glu, gub, sgu, sd, low, load_sems, store_sems, sem,
):
    step = pl.program_id(0)
    last = pl.num_programs(0) - 1
    slot = lax.rem(step, 2)
    other = 1 - slot
    after = jnp.minimum(step + 1, last)
    length = resid.shape[0]

    @pl.when(step == 0)
    def _():
        load_ffn(pos, packed, wgu.at[0], wd.at[0], load_sems.at[0], 0, 0, DT)

        def one(i, _):
            rows = pl.ds(pl.multiple_of(i * E, E), E)
            x = resid[rows, :]
            n = x * norm_rows(x) * gain[...]
            normed[rows, :] = n.astype(BF)
            normed_t[:, rows] = n.T.astype(BF)
            total[rows, :] = x
            normed_back[rows, :] = jnp.zeros_like(x)
            return 0

        lax.fori_loop(0, length // E, one, 0)

    wait_bytes(wgu.at[slot], load_sems.at[slot])
    wait_bytes(wd.at[slot], load_sems.at[slot])

    for c in range(length // HIGH_ROWS):
        rows = slice(c * HIGH_ROWS, (c + 1) * HIGH_ROWS)
        acts = mm(normed[rows, :], wgu[slot])
        glu_back = mm(back[rows, :], wd[slot], NT_DIMS)
        up = acts[:, FFN_BLOCK:]
        g, slope = gelu_pair(acts[:, :FFN_BLOCK])
        glu[rows, :] = (g * up).astype(BF)
        gub[rows, :FFN_BLOCK] = (glu_back * up * slope).astype(BF)
        gub[rows, FFN_BLOCK:] = (glu_back * g).astype(BF)

    for c in range(D // ROWS):
        cols = slice(c * ROWS, (c + 1) * ROWS)
        total[:, cols] += mm(glu[...], wd[slot, :, cols])
        normed_back[:, cols] += mm(gub[...], wgu[slot, cols, :], NT_DIMS)
        load_ffn(pos, packed, wgu.at[other], wd.at[other], load_sems.at[other], after, c * 2, 2)

    @pl.when(step >= 2)
    def _():
        wait_bytes(sgu.at[slot], store_sems.at[slot])
        wait_bytes(sd.at[slot], store_sems.at[slot])

    at = step * FFN_WIDE
    out_sem = store_sems.at[slot]
    sd[slot] = mm(glu[...], back[...], TN_DIMS).astype(BF)
    for c in range(DT):
        move_down(store_tile, pos, grads, sd.at[slot], out_sem, AT_DOWN + at * DT, c, FFN_WIDE)
    half = D // 2
    for c in range(2):
        rows = slice(c * half, (c + 1) * half)
        sgu[slot, rows, :] = mm(normed_t[rows, :], gub[...]).astype(BF)
        for j in range(DT // 2):
            firsts = (AT_GATE + at, AT_UP + at)
            move_pair(store_tile, pos, grads, sgu.at[slot], out_sem, firsts, FT, c * (DT // 2) + j, FFN_WIDE)

    @pl.when(step == last)
    def _():
        def one(i, gain_sum):
            rows = pl.ds(pl.multiple_of(i * E, E), E)
            x = resid[rows, :]
            n_back = normed_back[rows, :]
            inv = norm_rows(x)
            scaled = n_back * gain[...]
            mean = jnp.mean(scaled * x, axis=-1, keepdims=True)
            x_back = back[rows, :].astype(F32) + (inv * scaled - x * (inv * inv * inv * mean))
            normed_back[rows, :] = x_back
            normed[rows, :] = x_back.astype(BF)
            low[rows, :] = total[rows, :].astype(BF)
            return gain_sum + jnp.sum((n_back * x * inv).reshape(E // 8, 8, D), axis=0)

        gain_sum = lax.fori_loop(0, length // E, one, jnp.zeros((8, D), F32))
        gain_grad[...] = jnp.sum(gain_sum, axis=0, keepdims=True)
        outs = [
            pltpu.make_async_copy(normed_back, resid_back, sem.at[0]),
            pltpu.make_async_copy(normed, out_back, sem.at[1]),
            pltpu.make_async_copy(low, activation, sem.at[2]),
        ]
        for copy in outs:
            copy.start()
        for copy in outs:
            copy.wait()
        wait_bytes(wgu.at[other], load_sems.at[other])
        wait_bytes(wd.at[other], load_sems.at[other])
        for s in range(2):
            wait_bytes(sgu.at[s], store_sems.at[s])
            wait_bytes(sd.at[s], store_sems.at[s])


def ffn(pos, packed, resid, back, gain):
    length = resid.shape[0]
    return pl.pallas_call(
        ffn_kernel,
        grid_spec=pltpu.PrefetchScalarGridSpec(
            num_scalar_prefetch=1,
            grid=(F // FFN_BLOCK,),
            in_specs=[ANY, whole((length, D)), whole((length, D)), whole((1, D))],
            out_specs=[ANY, ANY, ANY, ANY, whole((1, D))],
            scratch_shapes=[
                pltpu.VMEM((length, D), BF),
                pltpu.VMEM((D, length), BF),
                pltpu.VMEM((length, D), F32),
                pltpu.VMEM((length, D), F32),
                pltpu.VMEM((2, D, 2 * FFN_BLOCK), BF),
                pltpu.VMEM((2, FFN_BLOCK, D), BF),
                pltpu.VMEM((length, FFN_BLOCK), BF),
                pltpu.VMEM((length, 2 * FFN_BLOCK), BF),
                pltpu.VMEM((2, D, 2 * FFN_BLOCK), BF),
                pltpu.VMEM((2, FFN_BLOCK, D), BF),
                pltpu.VMEM((length, D), BF),
                pltpu.SemaphoreType.DMA((2,)),
                pltpu.SemaphoreType.DMA((2,)),
                pltpu.SemaphoreType.DMA((3,)),
            ],
        ),
        out_shape=[
            jax.ShapeDtypeStruct(packed.shape, BF),
            jax.ShapeDtypeStruct((length, D), BF),
            jax.ShapeDtypeStruct((length, D), F32),
            jax.ShapeDtypeStruct((length, D), BF),
            jax.ShapeDtypeStruct((1, D), F32),
        ],
        compiler_params=pltpu.CompilerParams(vmem_limit_bytes=60 << 20),
        cost_estimate=pl.CostEstimate(
            flops=18 * length * D * F, bytes_accessed=110 << 20, transcendentals=length * F
        ),
        name="ffn_both_ways",
    )(pos, packed, resid, back, gain)


def temporal_backward_kernel(
    pos, packed, grads_in, resid_back, tokens, out_back, gain, params,
    branch, keep_in, u_in, p_in, q_in, ga_in, g_in, sg_in, conv_low, mixed,
    grads, input_grad, gain_grad, small_grad,
    normed_t, normed_back, wxy, wo, wri, bp, ri, mixed_back, conv_back, resid_rows,
    sxy, so, sri, zeros, load_sems, store_sems, zero_sem, resid_sems,
):
    step = pl.program_id(0)
    last = pl.num_programs(0) - 1
    slot = lax.rem(step, 2)
    other = 1 - slot
    after = jnp.minimum(step + 1, last)
    length = tokens.shape[0]
    chunks = length // CHUNK
    empty = pos.shape[0] - NT

    @pl.when(step == 0)
    def _():
        move_heads(load_tile, pos, packed, wri.at[0], load_sems.at[0], 0)
        load_xy(pos, packed, wxy.at[0], wo.at[0], load_sems.at[0], 0, 0, DT)
        zeros[...] = jnp.zeros_like(zeros)
        for t in range(empty):
            pltpu.make_async_copy(zeros.at[t], grads.at[pos[NT + t]], zero_sem).start()

        def one(i, _):
            rows = pl.ds(pl.multiple_of(i * E, E), E)
            x = tokens[rows, :].astype(F32)
            normed_t[:, rows] = (x * norm_rows(x) * gain[...]).T.astype(BF)
            normed_back[rows, :] = jnp.zeros_like(x)
            return 0

        lax.fori_loop(0, length // E, one, 0)
        wait_bytes(zeros, zero_sem)

    wait_xy(wxy.at[slot], wo.at[slot], wri.at[slot], load_sems.at[slot])
    move_heads(load_tile, pos, packed, wri.at[other], load_sems.at[other], after)
    values = params[...]

    for c in range(length // HIGH_ROWS):
        rows = slice(c * HIGH_ROWS, (c + 1) * HIGH_ROWS)
        mixed_back[rows, :] = mm(out_back[rows, :], wo[slot], NT_DIMS)
        half = DT // 2
        load_xy(pos, packed, wxy.at[other], wo.at[other], load_sems.at[other], after, c * half, half)
    row_in = lax.broadcasted_iota(jnp.int32, (CHUNK, BLOCK), 0)

    def fold(v):
        return jnp.sum(v.reshape(CHUNK // 8, 8, BLOCK), axis=0)

    def recur(i, kept):
        keep_after, carry, rec_sum, inp_sum, decay_sum = kept
        rows = pl.ds(pl.multiple_of((chunks - 1 - i) * CHUNK, CHUNK), CHUNK)
        keep = keep_in[rows, :]
        later = jnp.where(row_in == CHUNK - 1, keep_after, pltpu.roll(keep, CHUNK - 1, 0))
        m_back = mixed_back[rows, :]
        bp[rows, BLOCK:] = (m_back * sg_in[rows, :]).astype(BF)
        carried, carry = scan_chunk(later, m_back * g_in[rows, :], carry, True)
        rec_back = carried * p_in[rows, :]
        inp_back = carried * q_in[rows, :]
        conv_back[rows, :] = carried * ga_in[rows, :]
        for h in range(WIDE):
            at = h * 2 * E
            ri[rows, at : at + E] = rec_back[:, h * E : (h + 1) * E].astype(BF)
            ri[rows, at + E : at + 2 * E] = inp_back[:, h * E : (h + 1) * E].astype(BF)
        return (
            keep[0:1],
            carry,
            rec_sum + fold(rec_back),
            inp_sum + fold(inp_back),
            decay_sum + fold(carried * u_in[rows, :]),
        )

    one_row = jnp.zeros((1, BLOCK), F32)
    eight = jnp.zeros((8, BLOCK), F32)
    _, _, rec_sum, inp_sum, decay_sum = lax.fori_loop(
        0, chunks, recur, (one_row, one_row, eight, eight, eight), unroll=2
    )
    small_grad[5:6, :] = jnp.sum(rec_sum, axis=0, keepdims=True)
    small_grad[6:7, :] = jnp.sum(inp_sum, axis=0, keepdims=True)
    small_grad[7:8, :] = jnp.sum(decay_sum, axis=0, keepdims=True) * values[8:9]

    @pl.when(step >= 2)
    def _():
        wait_xy(sxy.at[slot], so.at[slot], sri.at[slot], store_sems.at[slot])

    for h in range(WIDE):
        part = slice(h * 2 * E, (h + 1) * 2 * E)
        one_head = slice(h * E, (h + 1) * E)
        conv_back[:, one_head] += mm(ri[:, part], wri[slot, h], NT_DIMS)
        sri[slot, h] = mm(conv_low[:, one_head], ri[:, part], TN_DIMS).astype(BF)

    def unconvolve(i, sums):
        r = pl.multiple_of(i * CHUNK, CHUNK)
        rows = pl.ds(r, CHUNK)
        back = conv_back[rows, :]
        after_rows = conv_back[pl.ds(pl.multiple_of(jnp.minimum(r + CHUNK, length - 8), 8), 8), :]
        ext = jnp.concatenate([back, jnp.where(i == chunks - 1, 0.0, after_rows)], axis=0)
        now = branch[rows, :]
        total = values[0:1] * back
        out = [sums[0] + fold(back * now)]
        for k in range(1, KW):
            total = total + values[k : k + 1] * ext[k : k + CHUNK]
        bp[rows, :BLOCK] = total.astype(BF)
        before = branch[pl.ds(pl.multiple_of(jnp.maximum(r - 8, 0), 8), 8), :]
        prev = jnp.concatenate([jnp.where(r == 0, 0.0, before), now], axis=0)
        for k in range(1, KW):
            out.append(sums[k] + fold(back * prev[8 - k : 8 - k + CHUNK]))
        out.append(sums[KW] + fold(back))
        return tuple(out)

    sums = lax.fori_loop(0, chunks, unconvolve, (eight,) * (KW + 1), unroll=4)
    for k in range(KW + 1):
        small_grad[k : k + 1, :] = jnp.sum(sums[k], axis=0, keepdims=True)

    for c in range(D // ROWS):
        cols = slice(c * ROWS, (c + 1) * ROWS)
        normed_back[:, cols] += mm(bp[...], wxy[slot, cols, :], NT_DIMS)

    at = step * WIDE
    out_sem = store_sems.at[slot]
    so[slot] = mm(mixed[...], out_back[...], TN_DIMS).astype(BF)
    for c in range(DT):
        move_down(store_tile, pos, grads, so.at[slot], out_sem, AT_OUT + at * DT, c)
    half = D // 2
    for c in range(2):
        rows = slice(c * half, (c + 1) * half)
        sxy[slot, rows, :] = mm(normed_t[rows, :], bp[...]).astype(BF)
        for j in range(DT // 2):
            firsts = (AT_X + at, AT_Y + at)
            move_pair(store_tile, pos, grads, sxy.at[slot], out_sem, firsts, RT, c * (DT // 2) + j)
    move_heads(store_tile, pos, grads, sri.at[slot], out_sem, step)

    @pl.when(step == last)
    def _():
        def fetch(i):
            return pltpu.make_async_copy(
                resid_back.at[pl.ds(i * E, E)], resid_rows.at[i % 2], resid_sems.at[i % 2]
            )

        fetch(0).start()
        gain_sum = jnp.zeros((8, D), F32)
        for i in range(length // E):
            if i + 1 < length // E:
                fetch(i + 1).start()
            fetch(i).wait()
            rows = slice(i * E, (i + 1) * E)
            x = tokens[rows, :].astype(F32)
            n_back = normed_back[rows, :]
            inv = norm_rows(x)
            scaled = n_back * gain[...]
            mean = jnp.mean(scaled * x, axis=-1, keepdims=True)
            x_back = resid_rows[i % 2] + (inv * scaled - x * (inv * inv * inv * mean))
            input_grad[rows, :] = x_back.astype(BF)
            gain_sum = gain_sum + jnp.sum((n_back * x * inv).reshape(E // 8, 8, D), axis=0)
        gain_grad[...] = jnp.sum(gain_sum, axis=0, keepdims=True)
        wait_xy(wxy.at[other], wo.at[other], wri.at[other], load_sems.at[other])
        for s in range(2):
            wait_xy(sxy.at[s], so.at[s], sri.at[s], store_sems.at[s])


def temporal_backward(pos, packed, grads, resid_back, tokens, out_back, gain, params, saved):
    length = tokens.shape[0]
    column = pl.BlockSpec((length, BLOCK), lambda i, *_: (0, i))
    return pl.pallas_call(
        temporal_backward_kernel,
        grid_spec=pltpu.PrefetchScalarGridSpec(
            num_scalar_prefetch=1,
            grid=(R // BLOCK,),
            in_specs=[
                ANY, ANY, ANY,
                whole((length, D)), whole((length, D)), whole((1, D)),
                pl.BlockSpec((16, BLOCK), lambda i, *_: (0, i)),
            ]
            + [column] * 10,
            out_specs=[
                ANY,
                whole((length, D)),
                whole((1, D)),
                pl.BlockSpec((8, BLOCK), lambda i, *_: (0, i)),
            ],
            scratch_shapes=[
                pltpu.VMEM((D, length), BF),
                pltpu.VMEM((length, D), F32),
                pltpu.VMEM((2, D, 2 * BLOCK), BF),
                pltpu.VMEM((2, BLOCK, D), BF),
                pltpu.VMEM((2, WIDE, E, 2 * E), BF),
                pltpu.VMEM((length, 2 * BLOCK), BF),
                pltpu.VMEM((length, 2 * BLOCK), BF),
                pltpu.VMEM((length, BLOCK), F32),
                pltpu.VMEM((length, BLOCK), F32),
                pltpu.VMEM((2, E, D), F32),
                pltpu.VMEM((2, D, 2 * BLOCK), BF),
                pltpu.VMEM((2, BLOCK, D), BF),
                pltpu.VMEM((2, WIDE, E, 2 * E), BF),
                pltpu.VMEM((pos.shape[0] - NT, E, E), BF),
                pltpu.SemaphoreType.DMA((2,)),
                pltpu.SemaphoreType.DMA((2,)),
                pltpu.SemaphoreType.DMA,
                pltpu.SemaphoreType.DMA((2,)),
            ],
        ),
        out_shape=[
            jax.ShapeDtypeStruct(grads.shape, BF),
            jax.ShapeDtypeStruct((length, D), BF),
            jax.ShapeDtypeStruct((1, D), F32),
            jax.ShapeDtypeStruct((8, R), F32),
        ],
        input_output_aliases={2: 0},
        compiler_params=pltpu.CompilerParams(vmem_limit_bytes=60 << 20),
        cost_estimate=pl.CostEstimate(
            flops=12 * length * D * R, bytes_accessed=130 << 20, transcendentals=length * R
        ),
        name="temporal_backward",
    )(pos, packed, grads, resid_back, tokens, out_back, gain, params, *saved)


def lanes_last(src, dst):
    count, lanes = src.shape[0], dst.shape[2]

    def one(q, _):
        at = pl.multiple_of(q * 8, 8)
        part = jnp.swapaxes(src[:, pl.ds(at, 8), :], 0, 1)
        if count < lanes:
            part = jnp.concatenate([part, jnp.zeros((8, lanes - count, E), F32)], axis=1)
        for k in range(8):
            dst[at + k] = part[k].T
        return 0

    lax.fori_loop(0, src.shape[1] // 8, one, 0)


def lanes_first(src, dst):
    count = dst.shape[0]

    def one(q, _):
        at = pl.multiple_of(q * 8, 8)
        part = jnp.swapaxes(src[:, pl.ds(at, 8), :], 0, 1)
        turned = jnp.stack([part[i].T[:count] for i in range(8)], axis=0)
        dst[:, pl.ds(at, 8), :] = jnp.swapaxes(turned, 0, 1)
        return 0

    lax.fori_loop(0, src.shape[1] // 8, one, 0)


def solve_kernel(gram, rows, left, right, factor, solved, inverse):
    size, tall = gram.shape[1], 32
    lanes_last(gram, factor)

    def eliminate(ref, acc, r0, count, j0, begin):
        window = pl.ds(r0, count)

        def one(k, acc):
            col = ref[k, window, :]
            return tuple(
                acc[c] - col * factor[k, j0 + c : j0 + c + 1, :] for c in range(8)
            )

        def eight(q, acc):
            for u in range(8):
                acc = one(q * 8 + u, acc)
            return acc

        return lax.fori_loop(begin // 8, j0 // 8, eight, acc)

    def finish(ref, acc, r0, count, j0, scales):
        acc = list(acc)
        for c in range(8):
            for c2 in range(c):
                acc[c] = acc[c] - acc[c2] * factor[j0 + c2, j0 + c : j0 + c + 1, :]
            acc[c] = acc[c] * scales[c]
            ref[j0 + c, pl.ds(r0, count), :] = acc[c]

    for j0 in range(0, size, 8):
        acc = tuple(factor[j0 + c, j0 : j0 + 8, :] for c in range(8))
        cols = list(eliminate(factor, acc, j0, 8, j0, 0))
        scales = []
        for c in range(8):
            pivot = cols[c][c : c + 1]
            scale = lax.rsqrt(pivot)
            scale = scale * (1.5 - 0.5 * (pivot * scale) * scale)
            scales.append(scale)
            cols[c] = cols[c] * scale
            for c2 in range(c + 1, 8):
                cols[c2] = cols[c2] - cols[c] * cols[c][c2 : c2 + 1]
        for c in range(8):
            factor[j0 + c, j0 : j0 + 8, :] = cols[c]
        at = j0 + 8
        while at < size:
            count = min(tall, size - at)
            acc = tuple(factor[j0 + c, at : at + count, :] for c in range(8))
            acc = eliminate(factor, acc, at, count, j0, 0)
            finish(factor, acc, at, count, j0, scales)
            at += count
        for at in range(0, size, tall):
            if at > j0:
                for c in range(8):
                    solved[j0 + c, at : at + tall, :] = jnp.zeros((tall, solved.shape[2]), F32)
                continue
            row = lax.broadcasted_iota(jnp.int32, (tall, solved.shape[2]), 0) + at
            acc = tuple(jnp.where(row == j0 + c, 1.0, 0.0) for c in range(8))
            acc = eliminate(solved, acc, at, tall, j0, at)
            finish(solved, acc, at, tall, j0, scales)

    lanes_first(solved, inverse)
    slots = left.shape[0]

    def one(m, _):
        for side, out in enumerate((left, right)):
            at = side * slots + m
            out[m] = product(split3(rows[at]), split3(inverse[at]), NN, 3)
        return 0

    lax.fori_loop(0, slots, one, 0, unroll=2 if slots % 2 == 0 else 1)


def solve(gram, rows):
    count = gram.shape[0]
    spare = -count % 8
    if spare:
        gram = jnp.pad(gram, ((0, spare), (0, 0), (0, 0)))
    lanes = E * -(-count // E)
    vmem = pl.BlockSpec(memory_space=pltpu.VMEM)
    shape = jax.ShapeDtypeStruct((count // 2, E, E), F32)
    return pl.pallas_call(
        solve_kernel,
        out_shape=[shape, shape],
        in_specs=[vmem, vmem],
        out_specs=[vmem, vmem],
        scratch_shapes=[
            pltpu.VMEM((E, E, lanes), F32),
            pltpu.VMEM((E, E, lanes), F32),
            pltpu.VMEM(gram.shape, F32),
        ],
        compiler_params=pltpu.CompilerParams(vmem_limit_bytes=56 << 20),
        cost_estimate=pl.CostEstimate(
            flops=60 * 10**9, bytes_accessed=12 * gram.size, transcendentals=0
        ),
        name="cholesky_solve",
    )(gram, rows)


def split3(x):
    one = x.astype(BF)
    rest = x - one.astype(F32)
    two = rest.astype(BF)
    return one, two, (rest - two.astype(F32)).astype(BF)


def product(left, right, dims, terms):
    pairs = [(a, t - a) for t in range(terms - 1, -1, -1) for a in range(t + 1)]
    pairs = [(a, b) for a, b in pairs if a < len(left) and b < len(right)]
    (left_axis,), (right_axis,) = dims[0]
    return mm(
        jnp.concatenate([left[a] for a, _ in pairs], axis=left_axis),
        jnp.concatenate([right[b] for _, b in pairs], axis=right_axis),
        dims,
    )


def rotate_kernel(
    own, weights, first, second, left, right, left_stat, right_stat, *refs
):
    weight_new, first_new, second_new, left_stat_new, right_stat_new, gram, rows = refs[-7:]
    each = range(own.shape[0])
    grads = [split3(own[i])[:2] for i in each]
    lefts = [split3(left[i]) for i in each]
    rights = [split3(right[i]) for i in each]
    sides = (
        (left_stat, left_stat_new, lefts, NT_DIMS),
        (right_stat, right_stat_new, rights, TN_DIMS),
    )
    halves = [split3(product(lefts[i][:2], grads[i], TN_DIMS, 2))[:2] for i in each]
    squares = [[product(grads[i], grads[i], side[3], 2) for i in each] for side in sides]
    turned = [product(halves[i], rights[i][:2], NN, 2) for i in each]
    moved = [[None for i in each] for side in sides]
    for s, (stat, stat_new, basis, _) in enumerate(sides):
        for i in each:
            now = BETA_STAT * stat[i] + (1.0 - BETA_STAT) * squares[s][i]
            stat_new[i] = now
            moved[s][i] = product(split3(now), basis[i], NN, 3)
            rows[s, i] = moved[s][i]
    scaled = []
    for i in each:
        first_now = BETA_ONE * first[i] + (1.0 - BETA_ONE) * turned[i]
        second_now = BETA_TWO * second[i] + (1.0 - BETA_TWO) * turned[i] * turned[i]
        first_new[i] = first_now
        second_new[i] = second_now
        scaled.append(
            first_now
            / (1.0 - BETA_ONE**STEP)
            / (jnp.sqrt(second_now / (1.0 - BETA_TWO**STEP)) + ADAM_EPS)
        )
    back = [split3(product(lefts[i][:2], split3(scaled[i])[:2], NN, 2))[:2] for i in each]
    for s in range(2):
        for i in each:
            pieces = split3(moved[s][i])
            gram[s, i] = product(pieces, pieces, TN_DIMS, 3)
    for i in each:
        update = product(back[i], rights[i][:2], NT_DIMS, 2)
        weight_new[i] = weights[i] - RATE * (update + DECAY * weights[i])


def rotate(own, spans, states, before):
    slots = states[0].shape[0]
    count = sum(n for _, n in spans)
    group = max(g for g in (1, 2, 4) if all(b % g == 0 and n % g == 0 for b, n in spans))
    begin, size = spans[0][0] // group, spans[0][1] // group
    other = spans[-1][0] // group - size if len(spans) > 1 else begin

    def place(i):
        return (jnp.where(i < size, i + begin, i + other), 0, 0)

    block = pl.BlockSpec((group, E, E), place)
    pair = pl.BlockSpec((2, group, E, E), lambda i: (0, *place(i)))
    one = jax.ShapeDtypeStruct((slots, E, E), F32)
    two = jax.ShapeDtypeStruct((2, slots, E, E), F32)
    return pl.pallas_call(
        rotate_kernel,
        grid=(count // group,),
        in_specs=[pl.BlockSpec((group, E, E), lambda i: (i, 0, 0))] + [block] * 7 + [ANY] * len(before),
        out_specs=[block] * 5 + [pair] * 2,
        out_shape=[one] * 5 + [two] * 2,
        input_output_aliases={8 + i: i for i in range(len(before))},
        compiler_params=pltpu.CompilerParams(vmem_limit_bytes=50 << 20),
        cost_estimate=pl.CostEstimate(
            flops=count * 10**9, bytes_accessed=16 * 4 * count * E * E, transcendentals=0
        ),
        name="rotate",
    )(own, *states, *before)


def small_step(grads, weights, first_vals, second_vals):
    first_new = BETA_ONE * first_vals + (1.0 - BETA_ONE) * grads
    second_new = BETA_TWO * second_vals + (1.0 - BETA_TWO) * grads * grads
    scaled = (
        first_new
        / (1.0 - BETA_ONE**STEP)
        / (jnp.sqrt(second_new / (1.0 - BETA_TWO**STEP)) + ADAM_EPS)
    )
    return (weights - SMALL_RATE * scaled, first_new, second_new)


def small_tile(small):
    lead = small.shape[:-1]
    pad = [(0, 0)] * len(lead) + [(0, E * E - small.shape[-1])]
    return jnp.pad(small, pad).reshape(*lead, E, E)


def swap_pairs(size, bit):
    return [(i, i ^ bit) for i in range(size)]


def split_bits(chips):
    bits = [1 << b for b in range(chips.bit_length() - 1)]
    return bits[: len(bits) // 2], bits[len(bits) // 2 :]


def part_sizes(per_device):
    first = max(1, round(per_device / 15)) * 4
    second = 2 * first
    return [first, second], per_device - first - second


def block_of(along, across, size, other, half):
    edge = jnp.where(
        (across == 0) & (along > 0), 2 * along if half == 0 else 2 * (other - 1 + along), 0
    )
    edge = jnp.where(
        (across > 0) & (along == 0),
        2 * (size - 1 + across) if half == 0 else 2 * across,
        edge,
    )
    inner = 2 * (size + other - 1) + half * (size - 1) * (other - 1)
    inner = inner + (across - 1) * (size - 1) + along - 1
    return jnp.where((across > 0) & (along > 0), inner, edge + half)


def place_of_tile(holder, inner, per_device, chips, cores, owners):
    z, core, chip = holder % owners, holder // owners % cores, holder // (owners * cores)
    low, high = split_bits(chips)
    width, height = 1 << len(low), 1 << len(high)
    far = chip ^ lax.axis_index("yx")
    x, y = far % width, far // width
    far_core = core ^ lax.axis_index("core")
    far_z = (z - lax.axis_index("owner")) % owners
    sizes, rest = part_sizes(per_device)
    total, at = jnp.zeros_like(inner), 0
    for size in sizes:
        side = size // 2
        for half in range(2):
            args = (x, y, width, height, 0) if half == 0 else (y, x, height, width, 1)
            block = far_core * (2 * chips) + block_of(*args)
            place = at * chips * cores * owners + (block * owners + far_z) * side
            begin = at + half * side
            here = (inner >= begin) & (inner < begin + side)
            total = jnp.where(here, place + inner - begin, total)
        at += size
    place = at * chips * cores * owners + ((far_core * owners + far_z) * chips + far) * rest
    return jnp.where(inner >= at, place + inner - at, total)


def add_low(a, b):
    return (a.astype(F32) + b.astype(F32)).astype(BF)


def to_core(x):
    return lax.ppermute(x, "core", [(0, 1), (1, 0)])


def to_chip(x, chips, bit):
    return lax.ppermute(x, "yx", swap_pairs(chips, bit))


RIGHT = [(0, 1), (1, 2), (2, 3)]
LEFT = [(1, 0), (2, 1), (3, 2)]


def hop_one(x):
    return lax.ppermute(x, "owner", LEFT), lax.ppermute(x, "owner", RIGHT)


def hop_two(near, z):
    from_right = lax.ppermute(near[0], "owner", LEFT[:2])
    from_left = lax.ppermute(near[1], "owner", RIGHT[1:])
    return jnp.where(z < 2, from_right, from_left)


def hop_three(middle):
    return lax.ppermute(middle, "owner", [(1, 0), (2, 3)])


def line_join(x, near, middle, ends, z):
    return [x, jnp.where(z == 3, ends, near[0]), middle, jnp.where(z == 0, ends, near[1])]


def halves_first(blocks):
    side = blocks[0].shape[0] // 2
    return jnp.concatenate([b[:side] for b in blocks] + [b[side:] for b in blocks], axis=0)


def butterfly(x, bits, chips):
    pieces = [x]
    for bit in bits:
        pieces = pieces + [to_chip(p, chips, bit) for p in pieces]
    return pieces[1:]


def tie(*trees):
    return lax.optimization_barrier(trees)


def spread_chunk(joined, low, high, chips):
    half = joined.shape[0] // 2
    along_x = butterfly(joined, low, chips)
    along_y = butterfly(joined, high, chips)
    return along_x, along_y, half


def spread_rest(along_x, along_y, half, low, high, chips):
    inner = []
    for p in along_y:
        inner += butterfly(p[:half], low, chips)
    for p in along_x:
        inner += butterfly(p[half:], high, chips)
    return inner


def put(buffer, pieces, at):
    for piece in pieces:
        buffer = lax.dynamic_update_slice(buffer, piece, (at, 0, 0))
        at += piece.shape[0]
    return buffer


def gather_tiles(mine, chips, devices, beside):
    z = lax.axis_index("owner")
    low, high = split_bits(chips)
    per_device = mine.shape[0]
    (first, second), rest = part_sizes(per_device)
    one, two, three = mine[:first], mine[first : first + second], mine[first + second :]
    buffer = blank(devices * per_device)

    def join(x, near, middle, ends):
        return halves_first(line_join(x, near, middle, ends, z))

    near = hop_one(one)
    three = jnp.concatenate([three] + butterfly(three, low + high, chips), axis=0)
    middle = hop_two(near, z)
    middle, three = tie(middle, three)
    one = join(one, near, middle, hop_three(middle))
    one, two = tie(one, two)

    along_x, along_y, half = spread_chunk(one, low, high, chips)
    near = hop_one(two)
    middle = hop_two(near, z)
    along_x, along_y, middle = tie(along_x, along_y, middle)
    inner = spread_rest(along_x, along_y, half, low, high, chips)
    two = join(two, near, middle, hop_three(middle))
    pieces_one = [one] + along_x + along_y + inner
    two, pieces_one, three, beside = tie(two, pieces_one, three, beside)

    along_x, along_y, half = spread_chunk(two, low, high, chips)
    near = hop_one(three)
    middle = hop_two(near, z)
    joined = jnp.concatenate(pieces_one, axis=0)
    along_x, along_y, middle, joined = tie(along_x, along_y, middle, joined)
    inner = spread_rest(along_x, along_y, half, low, high, chips)
    ends = hop_three(middle)
    far_one = to_core(joined)
    edge = [two] + along_x + along_y
    buffer = put(buffer, [joined], 0)
    buffer = put(buffer, edge, first * devices)
    inner, ends, edge, beside, buffer = tie(inner, ends, edge, beside, buffer)

    beside = lax.all_to_all(beside, AXES, split_axis=0, concat_axis=0, tiled=True)
    pieces_three = line_join(three, near, middle, ends, z)
    far_two = [to_core(p) for p in edge + inner]
    far_even = to_core(jnp.concatenate(pieces_three[::2], axis=0))
    far_odd = to_core(jnp.concatenate(pieces_three[1::2], axis=0))
    size = three.shape[0]
    far_three = [far_even[:size], far_odd[:size], far_even[size:], far_odd[size:]]
    buffer = put(buffer, [far_one], joined.shape[0])
    at = first * devices + sum(p.shape[0] for p in edge)
    buffer = put(buffer, inner + far_two, at)
    return put(buffer, pieces_three + far_three, (first + second) * devices), beside


def fold_butterfly(blocks, bits, chips):
    for bit in bits[::-1]:
        far = [to_chip(b, chips, bit) for b in blocks[len(blocks) // 2 :]]
        blocks = [add_low(a, b) for a, b in zip(blocks, far)]
    return blocks[0]


def fold_one(x, z):
    x = x.reshape(4, -1, E, E)
    far = lax.ppermute(jnp.where(z == 0, x[3], x[1]), "owner", [(0, 1), (3, 2)])
    return x, add_low(x[2], far)


def fold_two(state):
    x, middle = state
    from_left = lax.ppermute(middle, "owner", RIGHT[:2])
    from_right = lax.ppermute(middle, "owner", LEFT[1:])
    return x[0], add_low(x[1], from_left), add_low(x[3], from_right)


def fold_three(state, last):
    mine, right, left = state
    from_left = lax.ppermute(right, "owner", RIGHT)
    from_right = lax.ppermute(left, "owner", LEFT)
    total = mine.astype(F32) + from_left.astype(F32) + from_right.astype(F32)
    return total if last else total.astype(BF)


def edge_blocks(chips, low, high):
    return 2 * ((1 << len(low)) + (1 << len(high)) - 1)


def fold_inner(edge, inner, low, high, chips):
    width, height = 1 << len(low), 1 << len(high)
    half = edge.shape[0] // edge_blocks(chips, low, high)
    edge, inner = edge.reshape(-1, half, E, E), inner.reshape(-1, half, E, E)
    along_x = [edge[2 * i : 2 * i + 2] for i in range(width)]
    along_y = [edge[2 * (width - 1 + i) : 2 * (width - 1 + i) + 2] for i in range(1, height)]
    for i in range(1, height):
        begin = (i - 1) * (width - 1)
        old = along_y[i - 1]
        blocks = [old[0]] + [inner[begin + j] for j in range(width - 1)]
        along_y[i - 1] = jnp.stack([fold_butterfly(blocks, low, chips), old[1]])
    for i in range(1, width):
        begin = (width - 1) * (height - 1) + (i - 1) * (height - 1)
        blocks = [along_x[i][1]] + [inner[begin + j] for j in range(height - 1)]
        along_x[i] = jnp.stack([along_x[i][0], fold_butterfly(blocks, high, chips)])
    return along_x[0], along_x[1:], along_y


def fold_outer(state, low, high, chips, owners):
    own, along_x, along_y = state
    zero = jnp.zeros_like(own)
    from_x = fold_butterfly([zero] + along_x, low, chips)
    from_y = fold_butterfly([zero] + along_y, high, chips)
    x = own.astype(F32) + from_x.astype(F32) + from_y.astype(F32)
    x = x.astype(BF).reshape(2, owners, -1, E, E)
    return x.transpose(1, 0, 2, 3, 4).reshape(-1, E, E)


def scatter_tiles(grads, chips, devices, owners):
    z = lax.axis_index("owner")
    low, high = split_bits(chips)
    per_device = grads.shape[0] // devices
    (first, second), rest = part_sizes(per_device)

    def cut(begin, size):
        halfway = size * devices // 2
        edge = halfway // (2 * chips) * edge_blocks(chips, low, high)
        at = begin * devices
        cuts = [at, at + edge, at + halfway, at + halfway + edge, at + 2 * halfway]
        return [grads[a:b] for a, b in zip(cuts, cuts[1:])]

    one, two = cut(0, first), cut(first, second)
    three = grads[(first + second) * devices :].reshape(2, -1, E, E)

    got_inner = to_core(two[3])
    got_inner, far = tie(got_inner, two[2])
    got_edge = to_core(far)
    got_edge, far_one, far_three = tie(got_edge, one[2:], three[1])
    got_three, got_one = to_core(far_three), [to_core(x) for x in far_one]
    two_inner = add_low(two[1], got_inner)
    two = fold_inner(add_low(two[0], got_edge), two_inner, low, high, chips)
    three = fold_one(add_low(three[0], got_three), z)
    two, got_one = tie(two, got_one)

    two = fold_outer(two, low, high, chips, owners)
    three = fold_two(three)
    three = fold_three(three, False)
    two, three = tie(two, three)

    one = [add_low(a, b) for a, b in zip(one, got_one)]
    one = fold_inner(one[0], one[1], low, high, chips)
    two = fold_one(two, z)
    two = fold_two(two)
    one = fold_outer(one, low, high, chips, owners)
    two = fold_three(two, True)
    one, two = tie(one, two)

    blocks = list(three.reshape(chips, -1, E, E))
    bits = low + high
    for bit in bits[::-1]:
        moved = [to_chip(b, chips, bit) for b in blocks[len(blocks) // 2 :]]
        blocks = [
            a.astype(F32) + b.astype(F32) if bit == bits[0] else add_low(a, b)
            for a, b in zip(blocks, moved)
        ]
    one = fold_three(fold_two(fold_one(one, z)), True)
    return two, jnp.concatenate([one, blocks[0]], axis=0)


def blank_kernel(out):
    pass


def blank(count):
    return pl.pallas_call(
        blank_kernel,
        out_shape=jax.ShapeDtypeStruct((count, E, E), BF),
        out_specs=ANY,
        name="blank",
    )()


def body(
    inputs,
    cotangent,
    lengths,
    balance,
    owner_slot_tile,
    master,
    first_moment,
    second_moment,
    left_basis,
    right_basis,
    left_stat,
    right_stat,
    small_master,
    small_first,
    small_second,
):
    yx, cores, owners = (lax.axis_size(name) for name in AXES)
    devices = yx * cores * owners
    rank = lax.axis_index(AXES)
    tokens = inputs[0]
    seq_len = tokens.shape[0]
    held = master.shape[0]
    small_held = small_master.shape[0]
    per_device = held + 1

    place_args = (per_device, yx, cores, owners)

    slots = jnp.arange(owner_slot_tile.shape[0], dtype=jnp.int32)
    place = place_of_tile(slots // held, slots % held, *place_args)
    hit = owner_slot_tile[:, None] == slots[None, :]
    pos = jnp.sum(jnp.where(hit, place[:, None], 0), axis=0)
    ranks = jnp.arange(devices, dtype=jnp.int32)
    small_place = place_of_tile(ranks, jnp.full_like(ranks, held), *place_args)

    mine = jnp.concatenate([master.astype(BF), small_tile(small_master.astype(BF))[None]], axis=0)
    shares = cotangent.reshape(devices, seq_len // devices, D)
    mine, pos = tie(mine, pos)
    packed, spread = gather_tiles(mine, yx, devices, shares)

    used = -(-small_held // E)
    small = packed[:, :used][small_place].reshape(devices, used * E)[:, :small_held]
    small = small.reshape(-1).astype(F32)
    gain_one, gain_two = small[None, :D], small[None, D : 2 * D]
    wide = small[2 * D :].reshape(KW + 4, R)
    decay_log = wide[KW + 3]
    params = jnp.concatenate(
        [
            wide[: KW + 3],
            -8.0 * jax.nn.softplus(-decay_log)[None],
            8.0 * jax.nn.sigmoid(-decay_log)[None],
            jnp.zeros((16 - KW - 5, R), F32),
        ],
        axis=0,
    )

    place_of = jnp.sum(
        jnp.where(
            balance[:, None] == jnp.arange(devices, dtype=jnp.int32)[None, :],
            jnp.arange(devices, dtype=jnp.int32)[:, None],
            0,
        ),
        axis=0,
    )
    params, spread = tie(params, spread)
    back = lax.all_to_all(spread[place_of], AXES, split_axis=0, concat_axis=0, tiled=True)
    live = jnp.arange(seq_len, dtype=jnp.int32) < lengths[rank]
    back = jnp.where(live[:, None], back.reshape(seq_len, D), 0).astype(BF)

    saved, resid = temporal_forward(pos, packed, tokens, gain_one, params)
    grads, activation, resid_back, out_back, grad_gain_two = ffn(pos, packed, resid, back, gain_two)
    grads, input_grad, grad_gain_one, small_grad = temporal_backward(
        pos, packed, grads, resid_back, tokens, out_back, gain_one, params, saved
    )

    small_grads = jnp.concatenate(
        [grad_gain_one.reshape(-1), grad_gain_two.reshape(-1), small_grad.reshape(-1)], axis=0
    )
    small_tiles = small_tile(small_grads.reshape(devices, small_held)).astype(BF)
    grads = grads.at[small_place].set(small_tiles)
    own_two, own_one = scatter_tiles(grads, yx, devices, owners)
    own_small = own_one[-1].reshape(-1)[:small_held]

    (first, second), _ = part_sizes(per_device)
    states = (
        master, first_moment, second_moment, left_basis, right_basis, left_stat, right_stat
    )
    spans_two = [(first, second)]
    spans_one = [(0, first), (first + second, held - first - second)]
    news = rotate(own_two, spans_two, states, ())
    *news, gram, rows = rotate(own_one, spans_one, states, news)
    new_left, new_right = solve(gram.reshape(-1, E, E), rows.reshape(-1, E, E))
    new_master, new_first, new_second, new_left_stat, new_right_stat = news

    small_new, small_first_new, small_second_new = small_step(
        own_small, small_master, small_first, small_second
    )
    return (
        activation[None],
        input_grad[None],
        new_master,
        new_first,
        new_second,
        new_left,
        new_right,
        new_left_stat,
        new_right_stat,
        small_new,
        small_first_new,
        small_second_new,
    )


def solution(mesh):
    dp, owner = mesh.devices.shape
    fine = Mesh(mesh.devices.reshape(dp // 2, 2, owner), AXES)
    cut = P(AXES)
    return jax.shard_map(
        body,
        mesh=fine,
        in_specs=(cut, cut, P(), P(), P()) + (cut,) * 10,
        out_specs=(cut,) * 12,
        check_vma=False,
    )
```
